32 devices in a mesh: sub: 4 (over y, x), tm: 8 (over z, core).
Axes of the slice: x: 2, y: 2, z: 4, core: 2. Of those that a mesh axis runs over, the one named last changes fastest.
Arguments:
- streams: bfloat16 [2, 2160, 32768], P(None, 'sub', 'tm'), may hold values from -6 to 6
- beam_weights: bfloat16 [2, 100, 2160], P(None, None, 'sub'), may hold values from -0.09375 to 0.09375
- code_signs: int32 [32, 16], replicated, may hold values from 0 to 1
- gate_map: int32 [256], replicated, may hold values from 0 to 127, as said below
Outputs:
- profiles: float32 [128, 100, 128], P('tm', 'sub')
The draws below stay inside these ranges and needn't reach their ends.
Inputs may be any that keep to these rules, and one draw needn't show every extreme that they name: `gate_map`: each range gate is named by exactly 2 sections.
All inputs are finite; a program needn't handle non-finite values.
Results may differ from the reference program's by a relative error of at most 0.0041.
Values may be sent and summed in bfloat16 or wider, within the bound.
No kernel may reach another device: no remote copies, remote signals or barrier semaphores. Data moves between devices by JAX's collectives and lax.ppermute only.
A program may use at most 128 MiB of HBM per device.

```python
import math
import jax
import jax.numpy as jnp
from jax import lax

CH = 2160
BEAMS = 100
T_DEV = 4096
PKT = 32
IPP_LEN = 512
LAGS = 64
NCODES = 32
NBAUD = 16
BAUD_LEN = 8
SEC_LEN = 2
GATES = 128
NSEC = 256
TIME = 32768
REPS = 16
IPPS = 64
N_TM = 8


def draw_gate_map(key, part):
    order = jax.random.permutation(key, GATES)
    return order[jnp.arange(NSEC) % GATES].astype(jnp.int32)


def place_ends(result, own_key, smallest, high):
    place = [jax.random.randint(jax.random.fold_in(own_key, axis), (), 0, length) for axis, length in enumerate(result.shape)]
    longest = result.shape.index(max(result.shape))
    beside = place[:longest] + [(place[longest] + 1) % result.shape[longest]] + place[longest + 1:]
    return result.at[tuple(place)].set(smallest).at[tuple(beside)].set(high)


def block_levels(key, dims, cuts, smallest, top_value):
    gain = 1.0
    for dim, blocks in cuts:
        steps = jax.random.uniform(jax.random.fold_in(jax.random.fold_in(key, 6), dim), (blocks,), jnp.float32, smallest / len(cuts), top_value / len(cuts))
        gain = gain * jnp.repeat(jnp.exp(steps), dims[dim] // blocks).reshape((-1,) + (1,) * (len(dims) - 1 - dim))
    return gain


def scatter_about(key, extent, deviation, reach, shards=(), held_as=jnp.bfloat16):
    gain = block_levels(key, extent, shards, -0.22, 0.18) if shards else 1.0
    entries = jax.random.normal(key, extent, jnp.float32) * deviation * gain
    return jnp.minimum(jnp.maximum(entries, -reach), reach).astype(held_as)


def setup_inputs(seed: int = 0) -> dict:
    streams_of = jax.random.split(jax.random.key(seed), 5)
    return {
        "streams": scatter_about(streams_of[0], (2, CH, TIME), 1.0, 6.0, ((1, 4), (2, 8))),
        "beam_weights": scatter_about(streams_of[1], (2, BEAMS, CH), (2 * CH) ** -0.5, 0.09375, ((2, 4),)),
        "code_signs": place_ends(jax.random.randint(streams_of[2], (NCODES, NBAUD), 0, 2), jax.random.fold_in(streams_of[2], 1), 0, 1).astype(jnp.int32),
        "gate_map": draw_gate_map(jax.random.fold_in(streams_of[4], 71), 0),
    }


def complex_block(weights):
    w_real = weights[0]
    w_imag = weights[1]
    upper_rows = jnp.concatenate([w_real, -w_imag], 1)
    lower_rows = jnp.concatenate([w_imag, w_real], 1)
    return jnp.stack([upper_rows, lower_rows], 1).reshape(2 * w_real.shape[0], 2 * w_real.shape[1])

def lag_windows(segment):
    offsets = jnp.arange(1, LAGS + 1).astype(jnp.int32)
    return jax.vmap(lambda shift_by: lax.dynamic_slice_in_dim(segment, shift_by, IPP_LEN, 2), out_axes=2)(offsets)

def period_sections(segment, sequence):
    count = segment.shape[0]
    base = segment[:, :, :IPP_LEN]
    later = lag_windows(segment)
    base_real = base[:, 0][:, None, :]
    base_imag = base[:, 1][:, None, :]
    real_part = later[:, 0] * base_real + later[:, 1] * base_imag
    imag_part = later[:, 1] * base_real - later[:, 0] * base_imag
    offsets = jnp.arange(1, LAGS + 1).astype(jnp.int32)
    later_sign = jax.vmap(lambda shift_by: lax.dynamic_slice_in_dim(sequence, shift_by, IPP_LEN, 0))(offsets)
    decode = sequence[:IPP_LEN][None, :] * later_sign
    terms = jnp.stack([real_part, imag_part], 1) * decode[None, None, :, :]
    return terms.reshape(count, 2, LAGS, NSEC, SEC_LEN).sum(-1)

def reference(streams, beam_weights, code_signs, gate_map):
    block = complex_block(beam_weights)
    flat_rows = streams.reshape(2 * CH, TIME)

    def one_block(index):
        columns = lax.dynamic_slice_in_dim(flat_rows, index * T_DEV, T_DEV, 1)
        return jnp.dot(block, columns, preferred_element_type=jnp.float32).astype(jnp.bfloat16)
    arrival = lax.map(one_block, jnp.arange(N_TM).astype(jnp.int32))
    arrival = arrival.reshape(N_TM, BEAMS, 2, T_DEV).transpose(1, 2, 0, 3).reshape(BEAMS, 2, TIME)
    ordered = arrival.reshape(BEAMS, 2, N_TM, N_TM, REPS, PKT).transpose(0, 1, 3, 4, 2, 5).reshape(BEAMS, 2, TIME)
    extended = jnp.concatenate([ordered, jnp.zeros((BEAMS, 2, LAGS), jnp.bfloat16)], 2)
    positions = jnp.arange(IPP_LEN + LAGS)
    baud_hot = ((positions // BAUD_LEN % NBAUD)[:, None] == jnp.arange(NBAUD)[None, :]).astype(jnp.float32)
    sign_table = (2 * code_signs - 1).astype(jnp.float32)
    baud_seq = jnp.dot(sign_table, baud_hot.T, precision=lax.Precision.HIGHEST)

    def add_period(totals, period):
        start = (period * IPP_LEN).astype(jnp.int32)
        segment = lax.dynamic_slice_in_dim(extended, start, IPP_LEN + LAGS, 2).astype(jnp.float32)
        code = (period % NCODES).astype(jnp.int32)
        sequence = lax.dynamic_slice_in_dim(baud_seq, code, 1, 0)[0]
        return (totals + period_sections(segment, sequence), None)
    totals = jnp.zeros((BEAMS, 2, LAGS, NSEC), jnp.float32)
    totals, unused = lax.scan(add_period, totals, jnp.arange(IPPS).astype(jnp.int32))
    gate_hot = (gate_map[:, None] == jnp.arange(GATES)[None, :]).astype(jnp.float32)
    summed = jnp.dot(totals.reshape(BEAMS * 2 * LAGS, NSEC), gate_hot, precision=lax.Precision.HIGHEST)
    scale = 1.0 / math.sqrt(IPPS * IPP_LEN / GATES)
    return summed.reshape(BEAMS, 2 * LAGS, GATES).transpose(2, 0, 1) * scale
```

```python
import functools
import math

import jax
import jax.numpy as jnp
from jax import lax
from jax.experimental import pallas as pl
from jax.experimental.pallas import tpu as pltpu
from jax.sharding import PartitionSpec as P

PKT = 32
IPP_LEN = 512
LAGS = 64
NCODES = 32
BAUD_LEN = 8
SEC_LEN = 2
GATES = 128
LANES = 128
BLOCKS = IPP_LEN // LANES
PER_ROW = LANES // PKT
PKTS = IPP_LEN // PKT
STREAM_MAX = 6.0
WEIGHT_MAX = 0.09375
VMEM = 48 * 1024 * 1024
F32 = jnp.float32
BF16 = jnp.bfloat16


def beam_kernel(w_ref, x_ref, out_ref, first_ref, second_ref):
    beams = w_ref.shape[1]
    half = first_ref.shape[0] // 2

    @pl.when(pl.program_id(0) == 0)
    def _():
        first_ref[:beams] = w_ref[0]
        first_ref[half : half + beams] = w_ref[1]
        second_ref[:beams] = -w_ref[1]
        second_ref[half : half + beams] = w_ref[0]

    product = jnp.dot(first_ref[...], x_ref[0], preferred_element_type=F32)
    product += jnp.dot(second_ref[...], x_ref[1], preferred_element_type=F32)
    for row in range(out_ref.shape[2]):
        piece = product[:, row * LANES : (row + 1) * LANES]
        out_ref[0, :, row, :] = piece[:beams]
        out_ref[1, :, row, :] = piece[half : half + beams]


def partial_beams(streams, beam_weights):
    beams = beam_weights.shape[1]
    depth = streams.shape[1]
    samples = streams.shape[2]
    tile = 8 * LANES
    padded = (beams + 15) // 16 * 16
    return pl.pallas_call(
        beam_kernel,
        grid=(samples // tile,),
        in_specs=[
            pl.BlockSpec((2, beams, depth), lambda t: (0, 0, 0)),
            pl.BlockSpec((2, depth, tile), lambda t: (0, 0, t)),
        ],
        out_specs=pl.BlockSpec((2, beams, 8, LANES), lambda t: (0, 0, t, 0)),
        out_shape=jax.ShapeDtypeStruct((2, beams, samples // LANES, LANES), F32),
        scratch_shapes=[pltpu.VMEM((2 * padded, depth), BF16)] * 2,
        compiler_params=pltpu.CompilerParams(vmem_limit_bytes=VMEM),
        cost_estimate=pl.CostEstimate(
            flops=8 * beams * depth * samples,
            bytes_accessed=4 * depth * samples + 8 * beams * samples,
            transcendentals=0,
        ),
        name="partial_beams",
    )(beam_weights, streams)


def lag_kernel(scale, x_ref, sign_ref, gate_ref, out_ref):
    sources, slots, _, rows, _ = x_ref.shape
    row_groups = sign_ref.shape[0]
    depth = row_groups * rows
    lane = lax.broadcasted_iota(jnp.int32, (rows, LANES), 1)
    row = lax.broadcasted_iota(jnp.int32, (rows, LANES), 0)
    flip = (
        lax.broadcasted_iota(jnp.int32, (LANES, LANES), 0)
        + lax.broadcasted_iota(jnp.int32, (LANES, LANES), 1)
        == LANES - 1
    ).astype(F32).astype(BF16)
    real_lane = lax.broadcasted_iota(jnp.int32, (LANES, LANES), 1) < LAGS

    def columns_of(slot, part):
        pieces = [x_ref[d, slot, part].astype(F32) for d in range(sources)]
        raw = []
        for group in range(row_groups):
            blocks = []
            for block in range(BLOCKS):
                total = None
                for place in range(PER_ROW):
                    packet = group * PKTS + block * PER_ROW + place
                    shift = (place - packet // sources) * PKT % LANES
                    piece = pieces[packet % sources]
                    if shift:
                        piece = pltpu.roll(piece, shift, 1)
                    total = piece if total is None else jnp.where(lane >= place * PKT, piece, total)
                blocks.append(total)
            raw.append(blocks)
        last = jnp.where(row == rows - 1, 0.0, pltpu.roll(raw[0][0], rows - 1, 0))
        columns = []
        for block in range(BLOCKS):
            columns.append([raw[group][block] * sign_ref[group] for group in range(row_groups)])
        after = [raw[group + 1][0] for group in range(row_groups - 1)] + [last]
        columns.append([after[group] * sign_ref[group] for group in range(row_groups)])
        return [jnp.concatenate(column, 0).astype(BF16) for column in columns]

    for slot in range(slots):
        real = columns_of(slot, 0)
        imag = columns_of(slot, 1)
        both = [jnp.concatenate([a, b], 0) for a, b in zip(real, imag)]
        turned = [jnp.concatenate([b, -a], 0) for a, b in zip(real, imag)]
        total = jnp.zeros((GATES, LANES), F32)
        for block in range(BLOCKS):
            base = lax.dot_general(
                flip, both[block], (((1,), (1,)), ((), ())), preferred_element_type=F32
            ).astype(BF16)
            later = jnp.concatenate(
                [both[block], both[block + 1], turned[block], turned[block + 1]], 1
            )
            gram = jnp.dot(base, later, preferred_element_type=F32)
            real_lags = pltpu.roll(gram[:, : 2 * LANES], LANES, 1, stride=1, stride_axis=0)
            imag_lags = pltpu.roll(gram[:, 2 * LANES :], LANES + LAGS, 1, stride=1, stride_axis=0)
            lags = jnp.where(real_lane, real_lags[:, :LANES], imag_lags[:, :LANES])
            high = lags.astype(BF16)
            low = (lags - high.astype(F32)).astype(BF16)
            gate = gate_ref[:, block * LANES : (block + 1) * LANES]
            total += jnp.dot(gate, high, preferred_element_type=F32)
            total += jnp.dot(gate, low, preferred_element_type=F32)
        out_ref[:, slot] = (total * scale).reshape(out_ref.shape[0], -1, LANES)


def lag_profiles(series, signs, gate_hot, scale):
    sources, slots = series.shape[:2]
    return pl.pallas_call(
        functools.partial(lag_kernel, scale),
        out_shape=jax.ShapeDtypeStruct((sources, slots, GATES // sources, LANES), F32),
        compiler_params=pltpu.CompilerParams(vmem_limit_bytes=VMEM),
        name="lag_profiles",
    )(series, signs, gate_hot)


def sign_rows(code_signs, periods, row_groups):
    signs = jnp.repeat((2 * code_signs - 1).astype(F32), BAUD_LEN, axis=1)
    signs = jnp.tile(signs, (periods // NCODES, 1))
    return signs.reshape(periods // row_groups, row_groups, LANES).transpose(1, 0, 2)


def gate_rows(gate_map):
    position = jnp.arange(IPP_LEN)
    position = position // LANES * LANES + (LANES - 1 - position % LANES)
    gates = jnp.repeat(gate_map, SEC_LEN).reshape(BLOCKS, LANES)[:, ::-1].reshape(IPP_LEN)
    return (jnp.arange(GATES)[:, None] == gates[None, :]).astype(BF16)


def body(streams, beam_weights, code_signs, gate_map):
    groups = lax.axis_size("sub")
    sources = lax.axis_size("tm")
    beams = beam_weights.shape[1] // groups
    samples = streams.shape[2]
    slots = -(-beams // sources)
    periods = samples * sources // IPP_LEN
    here = lax.axis_index("sub")
    signs = sign_rows(code_signs, periods, sources // PER_ROW)
    gate_hot = gate_rows(gate_map)

    partial = partial_beams(streams, beam_weights)
    limit = 2 * streams.shape[1] * STREAM_MAX * WEIGHT_MAX
    gain = 2.0 ** math.floor(math.log2(60000.0 / limit))

    def block_of(group):
        return lax.dynamic_slice_in_dim(partial, group * beams, beams, 1)

    summed = block_of(here)
    for step in range(groups - 1, 0, -1):
        sent = (block_of(here ^ step) * gain).astype(jnp.float16)
        came = lax.ppermute(sent, "sub", [(i, i ^ step) for i in range(groups)])
        summed = summed + came.astype(F32) * (1.0 / gain)
    early = summed.astype(BF16).transpose(1, 0, 2, 3)
    early = jnp.pad(early, ((0, sources * slots - beams), (0, 0), (0, 0), (0, 0)))
    early = early.reshape((sources, slots) + early.shape[1:])
    series = lax.all_to_all(early, "tm", 0, 0, tiled=True)
    scale = 1.0 / math.sqrt(periods * IPP_LEN / GATES)
    term = lag_profiles(series, signs, gate_hot, scale)
    arrived = lax.all_to_all(term, "tm", 0, 0, tiled=True)
    arrived = arrived.reshape((sources * slots,) + arrived.shape[2:])
    return arrived[:beams].transpose(1, 0, 2)


def solution(mesh):
    placed = (P(None, "sub", "tm"), P(None, None, "sub"), P(), P())
    return jax.shard_map(
        body, mesh=mesh, in_specs=placed, out_specs=P("tm", "sub", None), check_vma=False
    )
```

```python
import functools
import math

import jax
import jax.numpy as jnp
from jax import lax
from jax.experimental import pallas as pl
from jax.experimental.pallas import tpu as pltpu
from jax.sharding import PartitionSpec as P

PKT = 32
IPP_LEN = 512
LAGS = 64
NCODES = 32
BAUD_LEN = 8
SEC_LEN = 2
GATES = 128
LANES = 128
BLOCKS = IPP_LEN // LANES
PER_ROW = LANES // PKT
PKTS = IPP_LEN // PKT
STREAM_MAX = 6.0
WEIGHT_MAX = 0.09375
VMEM = 48 * 1024 * 1024
CHUNKS = 1
F32 = jnp.float32
BF16 = jnp.bfloat16


def beam_kernel(w_ref, x_ref, out_ref):
    beams = out_ref.shape[1]
    depth, parts, samples = x_ref.shape
    product = jnp.dot(
        w_ref[...], x_ref[...].reshape(depth * parts, samples), preferred_element_type=F32
    )
    for row in range(out_ref.shape[2]):
        piece = product[:, row * LANES : (row + 1) * LANES]
        out_ref[0, :, row, :] = piece[:beams]
        out_ref[1, :, row, :] = piece[beams:]


def partial_beams(streams, weights, chunk, chunks):
    depth, _, samples = streams.shape
    beams = weights.shape[0] // 2
    tile = 8 * LANES
    tiles = samples // (tile * chunks)
    return pl.pallas_call(
        beam_kernel,
        grid=(tiles,),
        in_specs=[
            pl.BlockSpec(weights.shape, lambda t: (0, 0)),
            pl.BlockSpec((depth, 2, tile), lambda t: (0, 0, t + chunk * tiles)),
        ],
        out_specs=pl.BlockSpec((2, beams, 8, LANES), lambda t: (0, 0, t, 0)),
        out_shape=jax.ShapeDtypeStruct((2, beams, tiles * 8, LANES), F32),
        compiler_params=pltpu.CompilerParams(vmem_limit_bytes=VMEM),
        cost_estimate=pl.CostEstimate(
            flops=8 * beams * depth * samples // chunks,
            bytes_accessed=(4 * depth * samples + 8 * beams * samples) // chunks,
            transcendentals=0,
        ),
        name="partial_beams",
    )(weights, streams)


def mixed_weights(beam_weights):
    real = beam_weights[0]
    imag = beam_weights[1]
    rows = jnp.concatenate([jnp.stack([real, -imag], 2), jnp.stack([imag, real], 2)], 0)
    return rows.reshape(rows.shape[0], -1)


def lag_kernel(scale, count, place_ref, sign_ref, gate_ref, *refs):
    pieces_in = refs[:count]
    out_refs = refs[count:-2]
    x_ref, sum_ref = refs[-2:]
    sources, slots, _, rows, _ = x_ref.shape
    chips = len(out_refs)
    chunks = count // sources
    chip = place_ref[0]
    core = place_ref[1]
    taken = pieces_in[0].shape[0] - slots
    span = pieces_in[0].shape[2]
    for index, ref in enumerate(pieces_in):
        chunk, step, other = index // sources, index // 2 % chips, index % 2
        source = 2 * (chip ^ step) + (core ^ other)
        x_ref[source, :, :, chunk * span : (chunk + 1) * span] = ref[pl.ds(core * taken, slots)]
    row_groups = sign_ref.shape[0]
    lane = lax.broadcasted_iota(jnp.int32, (rows, LANES), 1)
    row = lax.broadcasted_iota(jnp.int32, (rows, LANES), 0)
    flip = (
        lax.broadcasted_iota(jnp.int32, (LANES, LANES), 0)
        + lax.broadcasted_iota(jnp.int32, (LANES, LANES), 1)
        == LANES - 1
    ).astype(F32).astype(BF16)
    real_lane = lax.broadcasted_iota(jnp.int32, (LANES, LANES), 1) < LAGS

    def columns_of(slot, part):
        pieces = [x_ref[d, slot, part].astype(F32) for d in range(sources)]
        raw = []
        for group in range(row_groups):
            blocks = []
            for block in range(BLOCKS):
                total = None
                for place in range(PER_ROW):
                    packet = group * PKTS + block * PER_ROW + place
                    shift = (place - packet // sources) * PKT % LANES
                    piece = pieces[packet % sources]
                    if shift:
                        piece = pltpu.roll(piece, shift, 1)
                    total = piece if total is None else jnp.where(lane >= place * PKT, piece, total)
                blocks.append(total)
            raw.append(blocks)
        last = jnp.where(row == rows - 1, 0.0, pltpu.roll(raw[0][0], rows - 1, 0))
        columns = []
        for block in range(BLOCKS):
            columns.append([raw[group][block] * sign_ref[group] for group in range(row_groups)])
        after = [raw[group + 1][0] for group in range(row_groups - 1)] + [last]
        columns.append([after[group] * sign_ref[group] for group in range(row_groups)])
        return [jnp.concatenate(column, 0).astype(BF16) for column in columns]

    for slot in range(slots):
        real = columns_of(slot, 0)
        imag = columns_of(slot, 1)
        both = [jnp.concatenate([a, b], 0) for a, b in zip(real, imag)]
        turned = [jnp.concatenate([b, -a], 0) for a, b in zip(real, imag)]
        total = jnp.zeros((GATES, LANES), F32)
        for block in range(BLOCKS):
            base = lax.dot_general(
                flip, both[block], (((1,), (1,)), ((), ())), preferred_element_type=F32
            ).astype(BF16)
            later = jnp.concatenate(
                [both[block], both[block + 1], turned[block], turned[block + 1]], 1
            )
            gram = jnp.dot(base, later, preferred_element_type=F32)
            real_lags = pltpu.roll(gram[:, : 2 * LANES], LANES, 1, stride=1, stride_axis=0)
            imag_lags = pltpu.roll(gram[:, 2 * LANES :], LANES + LAGS, 1, stride=1, stride_axis=0)
            lags = jnp.where(real_lane, real_lags[:, :LANES], imag_lags[:, :LANES])
            high = lags.astype(BF16)
            low = (lags - high.astype(F32)).astype(BF16)
            gate = gate_ref[:, block * LANES : (block + 1) * LANES]
            total += jnp.dot(gate, high, preferred_element_type=F32)
            total += jnp.dot(gate, low, preferred_element_type=F32)
        sum_ref[slot] = total * scale
    for step, out_ref in enumerate(out_refs):
        gates = out_ref.shape[1] * out_ref.shape[2]
        first = pl.multiple_of((chip ^ step) * gates, gates)
        out_ref[...] = sum_ref[:, pl.ds(first, gates), :].reshape(out_ref.shape)


def lag_profiles(place, signs, gate_hot, pieces, sources, slots, scale):
    chips = sources // 2
    rows = signs.shape[1]
    out = jax.ShapeDtypeStruct((slots, 2, GATES // sources, LANES), F32)
    vmem = pl.BlockSpec(memory_space=pltpu.VMEM)
    return pl.pallas_call(
        functools.partial(lag_kernel, scale, len(pieces)),
        in_specs=[pl.BlockSpec(memory_space=pltpu.SMEM)] + [vmem] * (2 + len(pieces)),
        out_specs=[vmem] * chips,
        out_shape=[out] * chips,
        scratch_shapes=[
            pltpu.VMEM((sources, slots, 2, rows, LANES), BF16),
            pltpu.VMEM((slots, GATES, LANES), F32),
        ],
        compiler_params=pltpu.CompilerParams(vmem_limit_bytes=VMEM),
        name="lag_profiles",
    )(place, signs, gate_hot, *pieces)


def gather_kernel(starts, width, place_ref, *refs):
    pieces_in = refs[:-2]
    out_ref, held_ref = refs[-2:]
    chips, _, slots = held_ref.shape[:3]
    chip = place_ref[0]
    core = place_ref[1]
    for index, ref in enumerate(pieces_in):
        held_ref[chip ^ (index // 2), core ^ (index % 2)] = ref[:, core]
    for beam in range(out_ref.shape[1]):
        owner = max(i for i in range(chips) if starts[i] <= beam)
        offset = beam - starts[owner]
        core_of = 0 if offset < slots else 1
        slot = offset - core_of * (width - slots)
        out_ref[:, beam, :] = held_ref[owner, core_of, slot]


def gather_beams(place, pieces, starts, width, beams):
    slots, _, gates, _ = pieces[0].shape
    vmem = pl.BlockSpec(memory_space=pltpu.VMEM)
    return pl.pallas_call(
        functools.partial(gather_kernel, starts, width),
        in_specs=[pl.BlockSpec(memory_space=pltpu.SMEM)] + [vmem] * len(pieces),
        out_specs=vmem,
        out_shape=jax.ShapeDtypeStruct((gates, beams, LANES), F32),
        scratch_shapes=[pltpu.VMEM((len(starts), 2, slots, gates, LANES), F32)],
        compiler_params=pltpu.CompilerParams(vmem_limit_bytes=VMEM),
        name="gather_beams",
    )(place, *pieces)


def sign_rows(code_signs, periods, row_groups):
    signs = jnp.repeat((2 * code_signs - 1).astype(F32), BAUD_LEN, axis=1)
    signs = jnp.tile(signs, (periods // NCODES, 1))
    return signs.reshape(periods // row_groups, row_groups, LANES).transpose(1, 0, 2)


def gate_rows(gate_map):
    position = jnp.arange(IPP_LEN)
    position = position // LANES * LANES + (LANES - 1 - position % LANES)
    gates = jnp.repeat(gate_map, SEC_LEN).reshape(BLOCKS, LANES)[:, ::-1].reshape(IPP_LEN)
    return (jnp.arange(GATES)[:, None] == gates[None, :]).astype(BF16)


def exchanged(block, axis, step):
    return lax.ppermute(block, axis, [(i, i ^ step) for i in range(lax.axis_size(axis))])


def spread(blocks):
    pieces = []
    for step, block in enumerate(blocks):
        block = exchanged(block, "tm", 2 * step) if step else block
        pieces += [block, exchanged(block, "tm", 1)]
    return pieces


def body(streams, beam_weights, code_signs, gate_map):
    groups = lax.axis_size("sub")
    sources = lax.axis_size("tm")
    chips = sources // 2
    beams = beam_weights.shape[1] // groups
    samples = streams.shape[2]
    width = -(-beams // chips)
    slots = -(-width // 2)
    starts = [i * (beams - width) // (chips - 1) for i in range(chips)]
    periods = samples * sources // IPP_LEN
    scale = 1.0 / math.sqrt(periods * IPP_LEN / GATES)
    here = lax.axis_index("sub")
    place = jnp.stack([lax.axis_index("tm") // 2, lax.axis_index("tm") % 2]).astype(jnp.int32)
    chip = place[0]
    signs = sign_rows(code_signs, periods, sources // PER_ROW)
    gate_hot = gate_rows(gate_map)
    weights = mixed_weights(beam_weights)
    limit = 2 * streams.shape[1] * STREAM_MAX * WEIGHT_MAX
    gain = 2.0 ** math.floor(math.log2(60000.0 / limit))
    by_channel = streams.transpose(1, 0, 2)

    pieces = []
    for chunk in range(CHUNKS):
        partial = partial_beams(by_channel, weights, chunk, CHUNKS)

        def block_of(group):
            return lax.dynamic_slice_in_dim(partial, group * beams, beams, 1)

        summed = block_of(here)
        for step in range(groups - 1, 0, -1):
            sent = (block_of(here ^ step) * gain).astype(jnp.float16)
            summed = summed + exchanged(sent, "sub", step).astype(F32) * (1.0 / gain)
        early = summed.astype(BF16).transpose(1, 0, 2, 3)
        blocks = []
        for step in range(chips):
            first = (chip ^ step) * (beams - width) // (chips - 1)
            blocks.append(lax.dynamic_slice_in_dim(early, first, width, 0))
        pieces += spread(blocks)
    terms = lag_profiles(place, signs, gate_hot, pieces, sources, slots, scale)
    return gather_beams(place, spread(terms), starts, width, beams)


def solution(mesh):
    placed = (P(None, "sub", "tm"), P(None, None, "sub"), P(), P())
    return jax.shard_map(
        body, mesh=mesh, in_specs=placed, out_specs=P("tm", "sub", None), check_vma=False
    )
```

```python
import functools
import math

import jax
import jax.numpy as jnp
from jax import lax
from jax.experimental import pallas as pl
from jax.experimental.pallas import tpu as pltpu
from jax.sharding import PartitionSpec as P

PKT = 32
IPP_LEN = 512
LAGS = 64
NCODES = 32
BAUD_LEN = 8
SEC_LEN = 2
GATES = 128
LANES = 128
BLOCKS = IPP_LEN // LANES
PER_ROW = LANES // PKT
PKTS = IPP_LEN // PKT
STREAM_MAX = 6.0
WEIGHT_MAX = 0.09375
VMEM = 48 * 1024 * 1024
CHUNKS = 2
F32 = jnp.float32
BF16 = jnp.bfloat16


def beam_kernel(w_ref, x_ref, out_ref, first_ref, second_ref, mixed_ref):
    beams, _, depth = w_ref.shape
    samples = x_ref.shape[2]
    rows = mixed_ref.shape[0]
    half = rows // 2

    @pl.when(pl.program_id(0) == 0)
    def _():
        first_ref[...] = jnp.zeros_like(first_ref)
        second_ref[...] = jnp.zeros_like(second_ref)
        weights = w_ref[...].astype(F32)
        real = weights[:, 0, :]
        imag = weights[:, 1, :]
        first_ref[:beams, :depth] = real
        first_ref[half : half + beams, :depth] = imag
        second_ref[:beams, :depth] = -imag
        second_ref[half : half + beams, :depth] = real
        source = lax.broadcasted_iota(jnp.int32, (2 * LANES, 2 * LANES), 0)
        target = lax.broadcasted_iota(jnp.int32, (2 * LANES, 2 * LANES), 1)
        weave = source % LANES * 2 + source // LANES == target
        weave = weave.astype(F32).astype(BF16)
        for block in range(first_ref.shape[1] // LANES):
            columns = slice(block * LANES, (block + 1) * LANES)
            pair = jnp.concatenate([first_ref[:, columns], second_ref[:, columns]], 1)
            woven = jnp.dot(pair.astype(BF16), weave, preferred_element_type=F32)
            mixed_ref[:, 2 * block * LANES : 2 * (block + 1) * LANES] = woven.astype(BF16)

    product = jnp.dot(
        mixed_ref[:, : 2 * depth],
        x_ref[...].reshape(2 * depth, samples),
        preferred_element_type=F32,
    )
    for row in range(out_ref.shape[2]):
        piece = product[:, row * LANES : (row + 1) * LANES]
        out_ref[0, :, row, :] = piece[:beams]
        out_ref[1, :, row, :] = piece[half : half + beams]


def partial_beams(streams, weights, chunk, chunks):
    depth, _, samples = streams.shape
    beams = weights.shape[0]
    tile = 8 * LANES
    tiles = samples // (tile * chunks)
    rows = 2 * (-(-beams // 8) * 8)
    columns = -(-depth // LANES) * LANES
    return pl.pallas_call(
        beam_kernel,
        grid=(tiles,),
        in_specs=[
            pl.BlockSpec(weights.shape, lambda t: (0, 0, 0)),
            pl.BlockSpec((depth, 2, tile), lambda t: (0, 0, t + chunk * tiles)),
        ],
        out_specs=pl.BlockSpec((2, beams, 8, LANES), lambda t: (0, 0, t, 0)),
        out_shape=jax.ShapeDtypeStruct((2, beams, tiles * 8, LANES), F32),
        scratch_shapes=[
            pltpu.VMEM((rows, columns), F32),
            pltpu.VMEM((rows, columns), F32),
            pltpu.VMEM((rows, 2 * columns), BF16),
        ],
        compiler_params=pltpu.CompilerParams(vmem_limit_bytes=VMEM),
        cost_estimate=pl.CostEstimate(
            flops=8 * beams * depth * samples // chunks,
            bytes_accessed=(4 * depth * samples + 8 * beams * samples) // chunks,
            transcendentals=0,
        ),
        name="partial_beams",
    )(weights, streams)


def lag_kernel(scale, count, place_ref, sign_ref, gate_ref, *refs):
    pieces_in = refs[:count]
    out_refs = refs[count:-2]
    x_ref, sum_ref = refs[-2:]
    sources, slots, _, rows, _ = x_ref.shape
    chips = len(out_refs)
    chunks = count // sources
    chip = place_ref[0]
    core = place_ref[1]
    taken = pieces_in[0].shape[0] - slots
    span = pieces_in[0].shape[2]
    for index, ref in enumerate(pieces_in):
        chunk, step, other = index // sources, index // 2 % chips, index % 2
        source = 2 * (chip ^ step) + (core ^ other)
        x_ref[source, :, :, chunk * span : (chunk + 1) * span] = ref[pl.ds(core * taken, slots)]
    row_groups = sign_ref.shape[0]
    lane = lax.broadcasted_iota(jnp.int32, (rows, LANES), 1)
    row = lax.broadcasted_iota(jnp.int32, (rows, LANES), 0)
    flip = (
        lax.broadcasted_iota(jnp.int32, (LANES, LANES), 0)
        + lax.broadcasted_iota(jnp.int32, (LANES, LANES), 1)
        == LANES - 1
    ).astype(F32).astype(BF16)
    real_lane = lax.broadcasted_iota(jnp.int32, (LANES, LANES), 1) < LAGS

    def columns_of(slot, part):
        pieces = [x_ref[d, slot, part].astype(F32) for d in range(sources)]
        raw = []
        for group in range(row_groups):
            blocks = []
            for block in range(BLOCKS):
                total = None
                for place in range(PER_ROW):
                    packet = group * PKTS + block * PER_ROW + place
                    shift = (place - packet // sources) * PKT % LANES
                    piece = pieces[packet % sources]
                    if shift:
                        piece = pltpu.roll(piece, shift, 1)
                    total = piece if total is None else jnp.where(lane >= place * PKT, piece, total)
                blocks.append(total)
            raw.append(blocks)
        last = jnp.where(row == rows - 1, 0.0, pltpu.roll(raw[0][0], rows - 1, 0))
        columns = []
        for block in range(BLOCKS):
            columns.append([raw[group][block] * sign_ref[group] for group in range(row_groups)])
        after = [raw[group + 1][0] for group in range(row_groups - 1)] + [last]
        columns.append([after[group] * sign_ref[group] for group in range(row_groups)])
        return [jnp.concatenate(column, 0).astype(BF16) for column in columns]

    for slot in range(slots):
        real = columns_of(slot, 0)
        imag = columns_of(slot, 1)
        both = [jnp.concatenate([a, b], 0) for a, b in zip(real, imag)]
        turned = [jnp.concatenate([b, -a], 0) for a, b in zip(real, imag)]
        total = jnp.zeros((GATES, LANES), F32)
        for block in range(BLOCKS):
            base = lax.dot_general(
                flip, both[block], (((1,), (1,)), ((), ())), preferred_element_type=F32
            ).astype(BF16)
            later = jnp.concatenate(
                [both[block], both[block + 1], turned[block], turned[block + 1]], 1
            )
            gram = jnp.dot(base, later, preferred_element_type=F32)
            real_lags = pltpu.roll(gram[:, : 2 * LANES], LANES, 1, stride=1, stride_axis=0)
            imag_lags = pltpu.roll(gram[:, 2 * LANES :], LANES + LAGS, 1, stride=1, stride_axis=0)
            lags = jnp.where(real_lane, real_lags[:, :LANES], imag_lags[:, :LANES])
            high = lags.astype(BF16)
            low = (lags - high.astype(F32)).astype(BF16)
            gate = gate_ref[:, block * LANES : (block + 1) * LANES]
            total += jnp.dot(gate, high, preferred_element_type=F32)
            total += jnp.dot(gate, low, preferred_element_type=F32)
        sum_ref[slot] = total * scale
    for step, out_ref in enumerate(out_refs):
        gates = out_ref.shape[1] * out_ref.shape[2]
        first = pl.multiple_of((chip ^ step) * gates, gates)
        out_ref[...] = sum_ref[:, pl.ds(first, gates), :].reshape(out_ref.shape).astype(BF16)


def lag_profiles(place, signs, gate_hot, pieces, sources, slots, scale):
    chips = sources // 2
    rows = signs.shape[1]
    out = jax.ShapeDtypeStruct((slots, 2, GATES // sources, LANES), BF16)
    vmem = pl.BlockSpec(memory_space=pltpu.VMEM)
    return pl.pallas_call(
        functools.partial(lag_kernel, scale, len(pieces)),
        in_specs=[pl.BlockSpec(memory_space=pltpu.SMEM)] + [vmem] * (2 + len(pieces)),
        out_specs=[vmem] * chips,
        out_shape=[out] * chips,
        scratch_shapes=[
            pltpu.VMEM((sources, slots, 2, rows, LANES), BF16),
            pltpu.VMEM((slots, GATES, LANES), F32),
        ],
        compiler_params=pltpu.CompilerParams(vmem_limit_bytes=VMEM),
        name="lag_profiles",
    )(place, signs, gate_hot, *pieces)


def gather_kernel(starts, width, place_ref, *refs):
    pieces_in = refs[:-2]
    out_ref, held_ref = refs[-2:]
    chips, _, slots = held_ref.shape[:3]
    chip = place_ref[0]
    core = place_ref[1]
    for index, ref in enumerate(pieces_in):
        held_ref[chip ^ (index // 2), core ^ (index % 2)] = ref[:, core].astype(F32)
    for beam in range(out_ref.shape[0]):
        owner = max(i for i in range(chips) if starts[i] <= beam)
        offset = beam - starts[owner]
        core_of = 0 if offset < slots else 1
        slot = offset - core_of * (width - slots)
        out_ref[beam] = held_ref[owner, core_of, slot]


def gather_beams(place, pieces, starts, width, beams):
    slots, _, gates, _ = pieces[0].shape
    vmem = pl.BlockSpec(memory_space=pltpu.VMEM)
    return pl.pallas_call(
        functools.partial(gather_kernel, starts, width),
        in_specs=[pl.BlockSpec(memory_space=pltpu.SMEM)] + [vmem] * len(pieces),
        out_specs=vmem,
        out_shape=jax.ShapeDtypeStruct((beams, gates, LANES), F32),
        scratch_shapes=[pltpu.VMEM((len(starts), 2, slots, gates, LANES), F32)],
        compiler_params=pltpu.CompilerParams(vmem_limit_bytes=VMEM),
        name="gather_beams",
    )(place, *pieces)


def sign_rows(code_signs, periods, row_groups):
    signs = jnp.repeat((2 * code_signs - 1).astype(F32), BAUD_LEN, axis=1)
    signs = jnp.tile(signs, (periods // NCODES, 1))
    return signs.reshape(periods // row_groups, row_groups, LANES).transpose(1, 0, 2)


def gate_rows(gate_map):
    position = jnp.arange(IPP_LEN)
    position = position // LANES * LANES + (LANES - 1 - position % LANES)
    gates = jnp.repeat(gate_map, SEC_LEN).reshape(BLOCKS, LANES)[:, ::-1].reshape(IPP_LEN)
    return (jnp.arange(GATES)[:, None] == gates[None, :]).astype(BF16)


def exchanged(block, axis, step):
    return lax.ppermute(block, axis, [(i, i ^ step) for i in range(lax.axis_size(axis))])


def spread(blocks):
    pieces = []
    for step, block in enumerate(blocks):
        block = exchanged(block, "tm", 2 * step) if step else block
        pieces += [block, exchanged(block, "tm", 1)]
    return pieces


def body(streams, beam_weights, code_signs, gate_map):
    groups = lax.axis_size("sub")
    sources = lax.axis_size("tm")
    chips = sources // 2
    beams = beam_weights.shape[1] // groups
    samples = streams.shape[2]
    width = -(-beams // chips)
    slots = -(-width // 2)
    starts = [i * (beams - width) // (chips - 1) for i in range(chips)]
    periods = samples * sources // IPP_LEN
    scale = 1.0 / math.sqrt(periods * IPP_LEN / GATES)
    here = lax.axis_index("sub")
    place = jnp.stack([lax.axis_index("tm") // 2, lax.axis_index("tm") % 2]).astype(jnp.int32)
    chip = place[0]
    signs = sign_rows(code_signs, periods, sources // PER_ROW)
    gate_hot = gate_rows(gate_map)
    weights = beam_weights.transpose(1, 0, 2)
    limit = 2 * streams.shape[1] * STREAM_MAX * WEIGHT_MAX
    gain = 2.0 ** math.floor(math.log2(60000.0 / limit))
    by_channel = streams.transpose(1, 0, 2)

    def block_of(array, group):
        return lax.dynamic_slice_in_dim(array, group * beams, beams, 1)

    pieces = []
    for chunk in range(CHUNKS):
        partial = partial_beams(by_channel, weights, chunk, CHUNKS)
        sent = []
        for step in range(groups - 1, 0, -1):
            sent.append((block_of(partial, here ^ step) * gain).astype(jnp.float16))
        *sent, weights = lax.optimization_barrier((*sent, weights))
        summed = block_of(partial, here)
        for step in range(groups - 1, 0, -1):
            came = exchanged(sent[groups - 1 - step], "sub", step)
            summed = summed + came.astype(F32) * (1.0 / gain)
        early = summed.astype(BF16).transpose(1, 0, 2, 3)
        blocks = []
        for step in range(chips):
            first = (chip ^ step) * (beams - width) // (chips - 1)
            blocks.append(lax.dynamic_slice_in_dim(early, first, width, 0))
        pieces += spread(blocks)
    terms = lag_profiles(place, signs, gate_hot, pieces, sources, slots, scale)
    return gather_beams(place, spread(terms), starts, width, beams).transpose(1, 0, 2)


def solution(mesh):
    placed = (P(None, "sub", "tm"), P(None, None, "sub"), P(), P())
    return jax.shard_map(
        body, mesh=mesh, in_specs=placed, out_specs=P("tm", "sub", None), check_vma=False
    )
```

```python
import functools
import math

import jax
import jax.numpy as jnp
from jax import lax
from jax.experimental import pallas as pl
from jax.experimental.pallas import tpu as pltpu
from jax.sharding import PartitionSpec as P

PKT = 32
IPP_LEN = 512
LAGS = 64
NCODES = 32
BAUD_LEN = 8
SEC_LEN = 2
GATES = 128
LANES = 128
BLOCKS = IPP_LEN // LANES
PER_ROW = LANES // PKT
PKTS = IPP_LEN // PKT
STREAM_MAX = 6.0
WEIGHT_MAX = 0.09375
VMEM = 48 * 1024 * 1024
CHUNKS = 2
SLICE = 8
F32 = jnp.float32
BF16 = jnp.bfloat16


def beam_kernel(first_column, w_hbm, x_hbm, out_ref, w_ref, x_ref, first_ref, second_ref, mixed_ref, sems):
    beams, _, depth = w_ref.shape
    slices, _, _, width = x_ref.shape
    half = mixed_ref.shape[0] // 2
    w_copy = pltpu.make_async_copy(w_hbm, w_ref, sems.at[slices])
    w_copy.start()
    copies = []
    for index in range(slices):
        columns = pl.ds(first_column + index * width, width)
        copies.append(
            pltpu.make_async_copy(x_hbm.at[:, :, columns], x_ref.at[index], sems.at[index])
        )
        copies[-1].start()
    first_ref[...] = jnp.zeros_like(first_ref)
    second_ref[...] = jnp.zeros_like(second_ref)
    source = lax.broadcasted_iota(jnp.int32, (2 * LANES, 2 * LANES), 0)
    target = lax.broadcasted_iota(jnp.int32, (2 * LANES, 2 * LANES), 1)
    weave = source % LANES * 2 + source // LANES == target
    weave = weave.astype(F32).astype(BF16)
    w_copy.wait()
    weights = w_ref[...].astype(F32)
    real = weights[:, 0, :]
    imag = weights[:, 1, :]
    first_ref[:beams, :depth] = real
    first_ref[half : half + beams, :depth] = imag
    second_ref[:beams, :depth] = -imag
    second_ref[half : half + beams, :depth] = real
    for block in range(first_ref.shape[1] // LANES):
        columns = slice(block * LANES, (block + 1) * LANES)
        pair = jnp.concatenate([first_ref[:, columns], second_ref[:, columns]], 1)
        woven = jnp.dot(pair.astype(BF16), weave, preferred_element_type=F32)
        mixed_ref[:, 2 * block * LANES : 2 * (block + 1) * LANES] = woven.astype(BF16)
    for index in range(slices):
        copies[index].wait()
        product = jnp.dot(
            mixed_ref[:, : 2 * depth],
            x_ref[index].reshape(2 * depth, width),
            preferred_element_type=F32,
        )
        rows = product.reshape(2 * half, width // LANES, LANES)
        place = slice(index * (width // LANES), (index + 1) * (width // LANES))
        out_ref[0, :, place, :] = rows[:beams]
        out_ref[1, :, place, :] = rows[half : half + beams]


def partial_beams(streams, weights, chunk, chunks):
    depth, _, samples = streams.shape
    beams = weights.shape[0]
    samples = samples // chunks
    width = SLICE * LANES
    rows = 2 * (-(-beams // 8) * 8)
    columns = -(-depth // LANES) * LANES
    return pl.pallas_call(
        functools.partial(beam_kernel, chunk * samples),
        in_specs=[pl.BlockSpec(memory_space=pltpu.HBM)] * 2,
        out_specs=pl.BlockSpec(memory_space=pltpu.VMEM),
        out_shape=jax.ShapeDtypeStruct((2, beams, samples // LANES, LANES), F32),
        scratch_shapes=[
            pltpu.VMEM(weights.shape, BF16),
            pltpu.VMEM((samples // width, depth, 2, width), BF16),
            pltpu.VMEM((rows, columns), F32),
            pltpu.VMEM((rows, columns), F32),
            pltpu.VMEM((rows, 2 * columns), BF16),
            pltpu.SemaphoreType.DMA((samples // width + 1,)),
        ],
        compiler_params=pltpu.CompilerParams(vmem_limit_bytes=VMEM),
        cost_estimate=pl.CostEstimate(
            flops=8 * beams * depth * samples,
            bytes_accessed=4 * depth * samples + 8 * beams * samples,
            transcendentals=0,
        ),
        name="partial_beams",
    )(weights, streams)


def lag_kernel(scale, count, place_ref, sign_ref, gate_ref, *refs):
    pieces_in = refs[:count]
    out_refs = refs[count:-4]
    x_ref, both_ref, lag_ref, sum_ref = refs[-4:]
    sources, slots, _, rows, _ = x_ref.shape
    chips = len(out_refs)
    chip = place_ref[0]
    core = place_ref[1]
    taken = pieces_in[0].shape[0] - slots
    span = pieces_in[0].shape[2]
    for index, ref in enumerate(pieces_in):
        chunk, step, other = index // sources, index // 2 % chips, index % 2
        source = 2 * (chip ^ step) + (core ^ other)
        x_ref[source, :, :, chunk * span : (chunk + 1) * span] = ref[pl.ds(core * taken, slots)]
    row_groups = sign_ref.shape[0]
    depth = row_groups * rows
    lane = lax.broadcasted_iota(jnp.int32, (rows, LANES), 1)
    row = lax.broadcasted_iota(jnp.int32, (rows, LANES), 0)
    flip = (
        lax.broadcasted_iota(jnp.int32, (LANES, LANES), 0)
        + lax.broadcasted_iota(jnp.int32, (LANES, LANES), 1)
        == LANES - 1
    ).astype(F32).astype(BF16)
    real_lane = lax.broadcasted_iota(jnp.int32, (LANES, LANES), 1) < LAGS
    real_depth = lax.broadcasted_iota(jnp.int32, (LANES, 2 * depth), 1) < depth

    def assemble(slot, part):
        loaded = [x_ref[d, slot, part].astype(F32) for d in range(sources)]
        raw = []
        for group in range(row_groups):
            blocks = []
            for block in range(BLOCKS):
                total = None
                for place in range(PER_ROW):
                    packet = group * PKTS + block * PER_ROW + place
                    shift = (place - packet // sources) * PKT % LANES
                    piece = loaded[packet % sources]
                    if shift:
                        piece = pltpu.roll(piece, shift, 1)
                    total = piece if total is None else jnp.where(lane >= place * PKT, piece, total)
                blocks.append(total)
            raw.append(blocks)
        raw.append([jnp.where(row == rows - 1, 0.0, pltpu.roll(raw[0][0], rows - 1, 0))])
        for group in range(row_groups):
            top = part * depth + group * rows
            for block in range(BLOCKS + 1):
                piece = raw[group][block] if block < BLOCKS else raw[group + 1][0]
                columns = slice(block * LANES, (block + 1) * LANES)
                both_ref[slot, top : top + rows, columns] = (piece * sign_ref[group]).astype(BF16)

    for slot in range(slots):
        assemble(slot, 0)
        assemble(slot, 1)
    for slot in range(slots):
        held = slice(slot * LANES, (slot + 1) * LANES)
        for block in range(BLOCKS):
            columns = slice(block * LANES, (block + 1) * LANES)
            base = lax.dot_general(
                flip,
                both_ref[slot, :, columns],
                (((1,), (1,)), ((), ())),
                preferred_element_type=F32,
            )
            swapped = pltpu.roll(base, depth, 1)
            turned = jnp.where(real_depth, -swapped, swapped)
            gram = jnp.dot(
                jnp.concatenate([base, turned], 0).astype(BF16),
                both_ref[slot, :, block * LANES : (block + 2) * LANES],
                preferred_element_type=F32,
            )
            real_lags = pltpu.roll(gram[:LANES], LANES, 1, stride=1, stride_axis=0)
            imag_lags = pltpu.roll(gram[LANES:], LANES + LAGS, 1, stride=1, stride_axis=0)
            lags = jnp.where(real_lane, real_lags[:, :LANES], imag_lags[:, :LANES])
            high = lags.astype(BF16)
            low = (lags - high.astype(F32)).astype(BF16)
            top = 2 * block * LANES
            lag_ref[top : top + LANES, held] = high
            lag_ref[top + LANES : top + 2 * LANES, held] = low
    gates = [gate_ref[:, b * LANES : (b + 1) * LANES] for b in range(BLOCKS)]
    gates = jnp.concatenate([gate for gate in gates for _ in range(2)], 1)
    sums = jnp.dot(gates, lag_ref[...], preferred_element_type=F32)
    for slot in range(slots):
        sum_ref[slot] = sums[:, slot * LANES : (slot + 1) * LANES] * scale
    for step, out_ref in enumerate(out_refs):
        gates = out_ref.shape[1] * out_ref.shape[2]
        first = pl.multiple_of((chip ^ step) * gates, gates)
        out_ref[...] = sum_ref[:, pl.ds(first, gates), :].reshape(out_ref.shape).astype(BF16)


def lag_profiles(place, signs, gate_hot, pieces, sources, slots, scale):
    chips = sources // 2
    row_groups, rows, _ = signs.shape
    out = jax.ShapeDtypeStruct((slots, 2, GATES // sources, LANES), BF16)
    vmem = pl.BlockSpec(memory_space=pltpu.VMEM)
    return pl.pallas_call(
        functools.partial(lag_kernel, scale, len(pieces)),
        in_specs=[pl.BlockSpec(memory_space=pltpu.SMEM)] + [vmem] * (2 + len(pieces)),
        out_specs=[vmem] * chips,
        out_shape=[out] * chips,
        scratch_shapes=[
            pltpu.VMEM((sources, slots, 2, rows, LANES), BF16),
            pltpu.VMEM((slots, 2 * row_groups * rows, (BLOCKS + 1) * LANES), BF16),
            pltpu.VMEM((2 * IPP_LEN, slots * LANES), BF16),
            pltpu.VMEM((slots, GATES, LANES), F32),
        ],
        compiler_params=pltpu.CompilerParams(vmem_limit_bytes=VMEM),
        name="lag_profiles",
    )(place, signs, gate_hot, *pieces)


def gather_kernel(width, place_ref, *refs):
    pieces_in = refs[:-1]
    out_ref = refs[-1]
    chips = len(pieces_in) // 2
    beams = out_ref.shape[0]
    slots = pieces_in[0].shape[0]
    chip = place_ref[0]
    core = place_ref[1]
    for index, ref in enumerate(pieces_in):
        first = (chip ^ (index // 2)) * (beams - width) // (chips - 1)
        first += (core ^ (index % 2)) * (width - slots)
        out_ref[pl.ds(first, slots)] = ref[:, core].astype(F32)


def gather_beams(place, pieces, width, beams):
    gates = pieces[0].shape[2]
    vmem = pl.BlockSpec(memory_space=pltpu.VMEM)
    return pl.pallas_call(
        functools.partial(gather_kernel, width),
        in_specs=[pl.BlockSpec(memory_space=pltpu.SMEM)] + [vmem] * len(pieces),
        out_specs=vmem,
        out_shape=jax.ShapeDtypeStruct((beams, gates, LANES), F32),
        compiler_params=pltpu.CompilerParams(vmem_limit_bytes=VMEM),
        name="gather_beams",
    )(place, *pieces)


def sign_rows(code_signs, periods, row_groups):
    signs = jnp.repeat((2 * code_signs - 1).astype(F32), BAUD_LEN, axis=1)
    signs = jnp.tile(signs, (periods // NCODES, 1))
    return signs.reshape(periods // row_groups, row_groups, LANES).transpose(1, 0, 2)


def gate_rows(gate_map):
    position = jnp.arange(IPP_LEN)
    position = position // LANES * LANES + (LANES - 1 - position % LANES)
    gates = jnp.repeat(gate_map, SEC_LEN).reshape(BLOCKS, LANES)[:, ::-1].reshape(IPP_LEN)
    return (jnp.arange(GATES)[:, None] == gates[None, :]).astype(BF16)


def exchanged(block, axis, step):
    return lax.ppermute(block, axis, [(i, i ^ step) for i in range(lax.axis_size(axis))])


def spread(blocks):
    pieces = []
    for step in reversed(range(len(blocks))):
        block = exchanged(blocks[step], "tm", 2 * step) if step else blocks[0]
        pieces = [block, exchanged(block, "tm", 1)] + pieces
    return pieces


def body(streams, beam_weights, code_signs, gate_map):
    groups = lax.axis_size("sub")
    sources = lax.axis_size("tm")
    chips = sources // 2
    beams = beam_weights.shape[1] // groups
    samples = streams.shape[2]
    width = -(-beams // chips)
    slots = -(-width // 2)
    periods = samples * sources // IPP_LEN
    scale = 1.0 / math.sqrt(periods * IPP_LEN / GATES)
    here = lax.axis_index("sub")
    place = jnp.stack([lax.axis_index("tm") // 2, lax.axis_index("tm") % 2]).astype(jnp.int32)
    chip = place[0]
    signs = sign_rows(code_signs, periods, sources // PER_ROW)
    gate_hot = gate_rows(gate_map)
    weights = pltpu.with_memory_space_constraint(beam_weights.transpose(1, 0, 2), pltpu.HBM)
    limit = 2 * streams.shape[1] * STREAM_MAX * WEIGHT_MAX
    gain = 2.0 ** math.floor(math.log2(60000.0 / limit))
    by_channel = streams.transpose(1, 0, 2)

    def block_of(array, group):
        return lax.dynamic_slice_in_dim(array, group * beams, beams, 1)

    pieces = []
    for chunk in range(CHUNKS):
        partial = partial_beams(by_channel, weights, chunk, CHUNKS)
        sent = []
        for step in range(groups - 1, 0, -1):
            sent.append((block_of(partial, here ^ step) * gain).astype(jnp.float16))
        *sent, weights = lax.optimization_barrier((*sent, weights))
        summed = block_of(partial, here)
        for step in range(groups - 1, 0, -1):
            came = exchanged(sent[groups - 1 - step], "sub", step)
            summed = summed + came.astype(F32) * (1.0 / gain)
        early = summed.astype(BF16).transpose(1, 0, 2, 3)
        blocks = []
        for step in range(chips):
            first = (chip ^ step) * (beams - width) // (chips - 1)
            blocks.append(lax.dynamic_slice_in_dim(early, first, width, 0))
        pieces += spread(blocks)
    terms = lag_profiles(place, signs, gate_hot, pieces, sources, slots, scale)
    return gather_beams(place, spread(terms), width, beams).transpose(1, 0, 2)


def solution(mesh):
    placed = (P(None, "sub", "tm"), P(None, None, "sub"), P(), P())
    return jax.shard_map(
        body, mesh=mesh, in_specs=placed, out_specs=P("tm", "sub", None), check_vma=False
    )
```

```python
import functools
import math

import jax
import jax.numpy as jnp
from jax import lax
from jax.experimental import pallas as pl
from jax.experimental.pallas import tpu as pltpu
from jax.sharding import PartitionSpec as P

PKT = 32
IPP_LEN = 512
LAGS = 64
NCODES = 32
BAUD_LEN = 8
SEC_LEN = 2
GATES = 128
LANES = 128
BLOCKS = IPP_LEN // LANES
PER_ROW = LANES // PKT
PKTS = IPP_LEN // PKT
STREAM_MAX = 6.0
WEIGHT_MAX = 0.09375
VMEM = 48 * 1024 * 1024
SLICE = 8
F32 = jnp.float32
BF16 = jnp.bfloat16


def beam_kernel(place_ref, w_hbm, x_hbm, *refs):
    out_refs = refs[:-6]
    w_ref, x_ref, first_ref, second_ref, mixed_ref, sems = refs[-6:]
    groups = len(out_refs)
    depth = w_ref.shape[2]
    slices, _, _, width = x_ref.shape
    half = mixed_ref.shape[0] // 2
    count = out_refs[0].shape[1]
    w_copy = pltpu.make_async_copy(w_hbm, w_ref, sems.at[slices])
    w_copy.start()
    copies = []
    for index in range(slices):
        columns = pl.ds(index * width, width)
        copies.append(
            pltpu.make_async_copy(x_hbm.at[:, :, columns], x_ref.at[index], sems.at[index])
        )
        copies[-1].start()
    first_ref[...] = jnp.zeros_like(first_ref)
    second_ref[...] = jnp.zeros_like(second_ref)
    source = lax.broadcasted_iota(jnp.int32, (2 * LANES, 2 * LANES), 0)
    target = lax.broadcasted_iota(jnp.int32, (2 * LANES, 2 * LANES), 1)
    weave = source % LANES * 2 + source // LANES == target
    weave = weave.astype(F32).astype(BF16)
    w_copy.wait()
    for group in range(groups):
        owner = place_ref[0] ^ group
        chosen = pl.ds(owner * (w_ref.shape[0] // groups) + place_ref[1], count)
        weights = w_ref[chosen].astype(F32)
        real = weights[:, 0, :]
        imag = weights[:, 1, :]
        top = group * count
        first_ref[top : top + count, :depth] = real
        first_ref[half + top : half + top + count, :depth] = imag
        second_ref[top : top + count, :depth] = -imag
        second_ref[half + top : half + top + count, :depth] = real
    for block in range(first_ref.shape[1] // LANES):
        columns = slice(block * LANES, (block + 1) * LANES)
        pair = jnp.concatenate([first_ref[:, columns], second_ref[:, columns]], 1)
        woven = jnp.dot(pair.astype(BF16), weave, preferred_element_type=F32)
        mixed_ref[:, 2 * block * LANES : 2 * (block + 1) * LANES] = woven.astype(BF16)
    for index in range(slices):
        copies[index].wait()
        product = jnp.dot(
            mixed_ref[:, : 2 * depth],
            x_ref[index].reshape(2 * depth, width),
            preferred_element_type=F32,
        )
        rows = product.reshape(2 * half, width // LANES, LANES)
        place = slice(index * (width // LANES), (index + 1) * (width // LANES))
        for group, out_ref in enumerate(out_refs):
            top = group * count
            out_ref[0, :, place, :] = rows[top : top + count]
            out_ref[1, :, place, :] = rows[half + top : half + top + count]


def partial_beams(streams, weights, place, groups, count):
    depth, _, samples = streams.shape
    beams = groups * count
    width = SLICE * LANES
    rows = 2 * (-(-beams // 8) * 8)
    columns = -(-depth // LANES) * LANES
    return pl.pallas_call(
        beam_kernel,
        in_specs=[pl.BlockSpec(memory_space=pltpu.SMEM)]
        + [pl.BlockSpec(memory_space=pltpu.HBM)] * 2,
        out_specs=[pl.BlockSpec(memory_space=pltpu.VMEM)] * groups,
        out_shape=[jax.ShapeDtypeStruct((2, count, samples // LANES, LANES), F32)] * groups,
        scratch_shapes=[
            pltpu.VMEM(weights.shape, BF16),
            pltpu.VMEM((samples // width, depth, 2, width), BF16),
            pltpu.VMEM((rows, columns), F32),
            pltpu.VMEM((rows, columns), F32),
            pltpu.VMEM((rows, 2 * columns), BF16),
            pltpu.SemaphoreType.DMA((samples // width + 1,)),
        ],
        compiler_params=pltpu.CompilerParams(vmem_limit_bytes=VMEM),
        cost_estimate=pl.CostEstimate(
            flops=8 * beams * depth * samples,
            bytes_accessed=4 * depth * samples + 8 * beams * samples,
            transcendentals=0,
        ),
        name="partial_beams",
    )(place, weights, streams)


def lag_kernel(scale, count, place_ref, sign_ref, gate_ref, *refs):
    pieces_in = refs[:count]
    out_refs = refs[count:-4]
    x_ref, both_ref, lag_ref, sum_ref = refs[-4:]
    sources, _, slots, rows, _ = x_ref.shape
    chip = place_ref[0]
    core = place_ref[1]
    taken = pieces_in[0].shape[1] - slots
    for index, ref in enumerate(pieces_in):
        source = 2 * (chip ^ (index // 2)) + (core ^ (index % 2))
        x_ref[source] = ref[:, pl.ds(core * taken, slots)]
    row_groups = sign_ref.shape[0]
    depth = row_groups * rows
    lane = lax.broadcasted_iota(jnp.int32, (rows, LANES), 1)
    row = lax.broadcasted_iota(jnp.int32, (rows, LANES), 0)
    flip = (
        lax.broadcasted_iota(jnp.int32, (LANES, LANES), 0)
        + lax.broadcasted_iota(jnp.int32, (LANES, LANES), 1)
        == LANES - 1
    ).astype(F32).astype(BF16)
    real_lane = lax.broadcasted_iota(jnp.int32, (LANES, LANES), 1) < LAGS
    real_depth = lax.broadcasted_iota(jnp.int32, (LANES, 2 * depth), 1) < depth

    def assemble(slot, part):
        loaded = [x_ref[d, part, slot].astype(F32) for d in range(sources)]
        raw = []
        for group in range(row_groups):
            blocks = []
            for block in range(BLOCKS):
                total = None
                for place in range(PER_ROW):
                    packet = group * PKTS + block * PER_ROW + place
                    shift = (place - packet // sources) * PKT % LANES
                    piece = loaded[packet % sources]
                    if shift:
                        piece = pltpu.roll(piece, shift, 1)
                    total = piece if total is None else jnp.where(lane >= place * PKT, piece, total)
                blocks.append(total)
            raw.append(blocks)
        raw.append([jnp.where(row == rows - 1, 0.0, pltpu.roll(raw[0][0], rows - 1, 0))])
        for group in range(row_groups):
            top = part * depth + group * rows
            for block in range(BLOCKS + 1):
                piece = raw[group][block] if block < BLOCKS else raw[group + 1][0]
                columns = slice(block * LANES, (block + 1) * LANES)
                both_ref[slot, top : top + rows, columns] = (piece * sign_ref[group]).astype(BF16)

    for slot in range(slots):
        assemble(slot, 0)
        assemble(slot, 1)
    for slot in range(slots):
        held = slice(slot * LANES, (slot + 1) * LANES)
        for block in range(BLOCKS):
            columns = slice(block * LANES, (block + 1) * LANES)
            base = lax.dot_general(
                flip,
                both_ref[slot, :, columns],
                (((1,), (1,)), ((), ())),
                preferred_element_type=F32,
            )
            swapped = pltpu.roll(base, depth, 1)
            turned = jnp.where(real_depth, -swapped, swapped)
            gram = jnp.dot(
                jnp.concatenate([base, turned], 0).astype(BF16),
                both_ref[slot, :, block * LANES : (block + 2) * LANES],
                preferred_element_type=F32,
            )
            real_lags = pltpu.roll(gram[:LANES], LANES, 1, stride=1, stride_axis=0)
            imag_lags = pltpu.roll(gram[LANES:], LANES + LAGS, 1, stride=1, stride_axis=0)
            lags = jnp.where(real_lane, real_lags[:, :LANES], imag_lags[:, :LANES])
            high = lags.astype(BF16)
            low = (lags - high.astype(F32)).astype(BF16)
            top = 2 * block * LANES
            lag_ref[top : top + LANES, held] = high
            lag_ref[top + LANES : top + 2 * LANES, held] = low
    gates = [gate_ref[:, b * LANES : (b + 1) * LANES] for b in range(BLOCKS)]
    gates = jnp.concatenate([gate for gate in gates for _ in range(2)], 1)
    sums = jnp.dot(gates, lag_ref[...], preferred_element_type=F32)
    for slot in range(slots):
        sum_ref[slot] = sums[:, slot * LANES : (slot + 1) * LANES] * scale
    for step, out_ref in enumerate(reversed(out_refs)):
        gates = out_ref.shape[1] * out_ref.shape[2]
        first = pl.multiple_of((chip ^ step) * gates, gates)
        out_ref[...] = sum_ref[:, pl.ds(first, gates), :].reshape(out_ref.shape).astype(BF16)


def lag_profiles(place, signs, gate_hot, pieces, sources, slots, scale):
    chips = sources // 2
    row_groups, rows, _ = signs.shape
    out = jax.ShapeDtypeStruct((slots, 2, GATES // sources, LANES), BF16)
    vmem = pl.BlockSpec(memory_space=pltpu.VMEM)
    return pl.pallas_call(
        functools.partial(lag_kernel, scale, len(pieces)),
        in_specs=[pl.BlockSpec(memory_space=pltpu.SMEM)] + [vmem] * (2 + len(pieces)),
        out_specs=[vmem] * chips,
        out_shape=[out] * chips,
        scratch_shapes=[
            pltpu.VMEM((sources, 2, slots, rows, LANES), BF16),
            pltpu.VMEM((slots, 2 * row_groups * rows, (BLOCKS + 1) * LANES), BF16),
            pltpu.VMEM((2 * IPP_LEN, slots * LANES), BF16),
            pltpu.VMEM((slots, GATES, LANES), F32),
        ],
        compiler_params=pltpu.CompilerParams(vmem_limit_bytes=VMEM),
        name="lag_profiles",
    )(place, signs, gate_hot, *pieces)


def gather_kernel(width, place_ref, *refs):
    pieces_in = refs[:-1]
    out_ref = refs[-1]
    chips = len(pieces_in) // 2
    beams = out_ref.shape[0]
    slots = pieces_in[0].shape[0]
    chip = place_ref[0]
    core = place_ref[1]
    for index, ref in enumerate(pieces_in):
        first = (chip ^ (index // 2)) * (beams - width) // (chips - 1)
        first += (core ^ (index % 2)) * (width - slots)
        out_ref[pl.ds(first, slots)] = ref[:, core].astype(F32)


def gather_beams(place, pieces, width, beams):
    gates = pieces[0].shape[2]
    vmem = pl.BlockSpec(memory_space=pltpu.VMEM)
    return pl.pallas_call(
        functools.partial(gather_kernel, width),
        in_specs=[pl.BlockSpec(memory_space=pltpu.SMEM)] + [vmem] * len(pieces),
        out_specs=vmem,
        out_shape=jax.ShapeDtypeStruct((beams, gates, LANES), F32),
        compiler_params=pltpu.CompilerParams(vmem_limit_bytes=VMEM),
        name="gather_beams",
    )(place, *pieces)


def sign_rows(code_signs, periods, row_groups):
    signs = jnp.repeat((2 * code_signs - 1).astype(F32), BAUD_LEN, axis=1)
    signs = jnp.tile(signs, (periods // NCODES, 1))
    return signs.reshape(periods // row_groups, row_groups, LANES).transpose(1, 0, 2)


def gate_rows(gate_map):
    position = jnp.arange(IPP_LEN)
    position = position // LANES * LANES + (LANES - 1 - position % LANES)
    gates = jnp.repeat(gate_map, SEC_LEN).reshape(BLOCKS, LANES)[:, ::-1].reshape(IPP_LEN)
    return (jnp.arange(GATES)[:, None] == gates[None, :]).astype(BF16)


def exchanged(block, axis, step):
    return lax.ppermute(block, axis, [(i, i ^ step) for i in range(lax.axis_size(axis))])


def spread(blocks):
    pieces = []
    for step, block in enumerate(blocks):
        block = exchanged(block, "tm", 2 * step) if step else block
        pieces += [block, exchanged(block, "tm", 1)]
    return pieces


def body(streams, beam_weights, code_signs, gate_map):
    groups = lax.axis_size("sub")
    sources = lax.axis_size("tm")
    chips = sources // 2
    beams = beam_weights.shape[1] // groups
    samples = streams.shape[2]
    width = -(-beams // chips)
    slots = -(-width // 2)
    periods = samples * sources // IPP_LEN
    scale = 1.0 / math.sqrt(periods * IPP_LEN / GATES)
    here = lax.axis_index("sub")
    place = jnp.stack([lax.axis_index("tm") // 2, lax.axis_index("tm") % 2]).astype(jnp.int32)
    chip = place[0]
    signs = sign_rows(code_signs, periods, sources // PER_ROW)
    gate_hot = gate_rows(gate_map)
    weights = pltpu.with_memory_space_constraint(beam_weights.transpose(1, 0, 2), pltpu.HBM)
    limit = 2 * streams.shape[1] * STREAM_MAX * WEIGHT_MAX
    gain = 2.0 ** math.floor(math.log2(60000.0 / limit))
    by_channel = streams.transpose(1, 0, 2)

    def first_of(owner):
        return owner * (beams - width) // (chips - 1)

    half = chips // 2
    count = max((half - 1) * (beams - width) // (chips - 1) + width, beams - first_of(half))
    low = chip < half
    blocks = [None] * chips
    for far in (True, False):
        start = jnp.where(low == far, beams - count, 0).astype(jnp.int32)
        chosen = jnp.stack([here, start]).astype(jnp.int32)
        partial = partial_beams(by_channel, weights, chosen, groups, count)
        total = partial[0]
        for step in range(groups - 1, 0, -1):
            came = exchanged((partial[step] * gain).astype(jnp.float16), "sub", step)
            total = total + came.astype(F32) * (1.0 / gain)
        total = total.astype(BF16)
        for step in range(half, chips) if far else range(half):
            place_of = first_of(chip ^ step) - start
            blocks[step] = lax.dynamic_slice_in_dim(total, place_of, width, 1)
    terms = lag_profiles(place, signs, gate_hot, spread(blocks), sources, slots, scale)
    return gather_beams(place, spread(terms[::-1]), width, beams).transpose(1, 0, 2)


def solution(mesh):
    placed = (P(None, "sub", "tm"), P(None, None, "sub"), P(), P())
    return jax.shard_map(
        body, mesh=mesh, in_specs=placed, out_specs=P("tm", "sub", None), check_vma=False
    )
```

```python
import functools
import math

import jax
import jax.numpy as jnp
from jax import lax
from jax.experimental import pallas as pl
from jax.experimental.pallas import tpu as pltpu
from jax.sharding import PartitionSpec as P

PKT = 32
IPP_LEN = 512
LAGS = 64
NCODES = 32
BAUD_LEN = 8
SEC_LEN = 2
GATES = 128
LANES = 128
BLOCKS = IPP_LEN // LANES
PER_ROW = LANES // PKT
PKTS = IPP_LEN // PKT
STREAM_MAX = 6.0
WEIGHT_MAX = 0.09375
VMEM = 48 * 1024 * 1024
SLICE = 8
F32 = jnp.float32
BF16 = jnp.bfloat16


def beam_kernel(here_ref, start_ref, w_hbm, x_hbm, *refs):
    out_refs = refs[:-6]
    w_ref, x_ref, first_ref, second_ref, mixed_ref, sems = refs[-6:]
    groups = len(out_refs)
    depth = w_ref.shape[2]
    slices, _, _, width = x_ref.shape
    half = mixed_ref.shape[0] // 2
    count = out_refs[0].shape[1]
    w_copy = pltpu.make_async_copy(w_hbm, w_ref, sems.at[slices])
    w_copy.start()
    copies = []
    for index in range(slices):
        columns = pl.ds(index * width, width)
        copies.append(
            pltpu.make_async_copy(x_hbm.at[:, :, columns], x_ref.at[index], sems.at[index])
        )
        copies[-1].start()
    first_ref[...] = jnp.zeros_like(first_ref)
    second_ref[...] = jnp.zeros_like(second_ref)
    source = lax.broadcasted_iota(jnp.int32, (2 * LANES, 2 * LANES), 0)
    target = lax.broadcasted_iota(jnp.int32, (2 * LANES, 2 * LANES), 1)
    weave = source % LANES * 2 + source // LANES == target
    weave = weave.astype(F32).astype(BF16)
    w_copy.wait()
    for group in range(groups):
        owner = here_ref[0] ^ group
        chosen = pl.ds(owner * (w_ref.shape[0] // groups) + start_ref[0], count)
        weights = w_ref[chosen].astype(F32)
        real = weights[:, 0, :]
        imag = weights[:, 1, :]
        top = group * count
        first_ref[top : top + count, :depth] = real
        first_ref[half + top : half + top + count, :depth] = imag
        second_ref[top : top + count, :depth] = -imag
        second_ref[half + top : half + top + count, :depth] = real
    for block in range(first_ref.shape[1] // LANES):
        columns = slice(block * LANES, (block + 1) * LANES)
        pair = jnp.concatenate([first_ref[:, columns], second_ref[:, columns]], 1)
        woven = jnp.dot(pair.astype(BF16), weave, preferred_element_type=F32)
        mixed_ref[:, 2 * block * LANES : 2 * (block + 1) * LANES] = woven.astype(BF16)
    for index in range(slices):
        copies[index].wait()
        product = jnp.dot(
            mixed_ref[:, : 2 * depth],
            x_ref[index].reshape(2 * depth, width),
            preferred_element_type=F32,
        )
        rows = product.reshape(2 * half, width // LANES, LANES)
        place = slice(index * (width // LANES), (index + 1) * (width // LANES))
        for group, out_ref in enumerate(out_refs):
            top = group * count
            out_ref[0, :, place, :] = rows[top : top + count]
            out_ref[1, :, place, :] = rows[half + top : half + top + count]


def partial_beams(streams, weights, here, start, groups, count):
    depth, _, samples = streams.shape
    beams = groups * count
    width = SLICE * LANES
    rows = 2 * (-(-beams // 8) * 8)
    columns = -(-depth // LANES) * LANES
    return pl.pallas_call(
        beam_kernel,
        in_specs=[pl.BlockSpec(memory_space=pltpu.SMEM)] * 2
        + [pl.BlockSpec(memory_space=pltpu.HBM)] * 2,
        out_specs=[pl.BlockSpec(memory_space=pltpu.VMEM)] * groups,
        out_shape=[jax.ShapeDtypeStruct((2, count, samples // LANES, LANES), F32)] * groups,
        scratch_shapes=[
            pltpu.VMEM(weights.shape, BF16),
            pltpu.VMEM((samples // width, depth, 2, width), BF16),
            pltpu.VMEM((rows, columns), F32),
            pltpu.VMEM((rows, columns), F32),
            pltpu.VMEM((rows, 2 * columns), BF16),
            pltpu.SemaphoreType.DMA((samples // width + 1,)),
        ],
        compiler_params=pltpu.CompilerParams(vmem_limit_bytes=VMEM),
        cost_estimate=pl.CostEstimate(
            flops=8 * beams * depth * samples,
            bytes_accessed=4 * depth * samples + 8 * beams * samples,
            transcendentals=0,
        ),
        name="partial_beams",
    )(here.reshape(1), start.reshape(1), weights, streams)


def lag_kernel(scale, count, chip_ref, core_ref, sign_ref, gate_ref, *refs):
    pieces_in = refs[:count]
    out_refs = refs[count:-4]
    x_ref, both_ref, lag_ref, sum_ref = refs[-4:]
    sources, _, slots, rows, _ = x_ref.shape
    chip = chip_ref[0]
    core = core_ref[0]
    taken = pieces_in[0].shape[1] - slots
    for index, ref in enumerate(pieces_in):
        source = 2 * (chip ^ (index // 2)) + (core ^ (index % 2))
        x_ref[source] = ref[:, pl.ds(core * taken, slots)]
    row_groups = sign_ref.shape[0]
    depth = row_groups * rows
    lane = lax.broadcasted_iota(jnp.int32, (rows, LANES), 1)
    row = lax.broadcasted_iota(jnp.int32, (rows, LANES), 0)
    flip = (
        lax.broadcasted_iota(jnp.int32, (LANES, LANES), 0)
        + lax.broadcasted_iota(jnp.int32, (LANES, LANES), 1)
        == LANES - 1
    ).astype(F32).astype(BF16)
    real_lane = lax.broadcasted_iota(jnp.int32, (LANES, LANES), 1) < LAGS
    real_depth = lax.broadcasted_iota(jnp.int32, (LANES, 2 * depth), 1) < depth

    def assemble(slot, part):
        loaded = [x_ref[d, part, slot].astype(F32) for d in range(sources)]
        raw = []
        for group in range(row_groups):
            blocks = []
            for block in range(BLOCKS):
                total = None
                for place in range(PER_ROW):
                    packet = group * PKTS + block * PER_ROW + place
                    shift = (place - packet // sources) * PKT % LANES
                    piece = loaded[packet % sources]
                    if shift:
                        piece = pltpu.roll(piece, shift, 1)
                    total = piece if total is None else jnp.where(lane >= place * PKT, piece, total)
                blocks.append(total)
            raw.append(blocks)
        raw.append([jnp.where(row == rows - 1, 0.0, pltpu.roll(raw[0][0], rows - 1, 0))])
        for group in range(row_groups):
            top = part * depth + group * rows
            for block in range(BLOCKS + 1):
                piece = raw[group][block] if block < BLOCKS else raw[group + 1][0]
                columns = slice(block * LANES, (block + 1) * LANES)
                both_ref[slot, top : top + rows, columns] = (piece * sign_ref[group]).astype(BF16)

    for slot in range(slots):
        assemble(slot, 0)
        assemble(slot, 1)
    for slot in range(slots):
        held = slice(slot * LANES, (slot + 1) * LANES)
        for block in range(BLOCKS):
            columns = slice(block * LANES, (block + 1) * LANES)
            base = lax.dot_general(
                flip,
                both_ref[slot, :, columns],
                (((1,), (1,)), ((), ())),
                preferred_element_type=F32,
            )
            swapped = pltpu.roll(base, depth, 1)
            turned = jnp.where(real_depth, -swapped, swapped)
            gram = jnp.dot(
                jnp.concatenate([base, turned], 0).astype(BF16),
                both_ref[slot, :, block * LANES : (block + 2) * LANES],
                preferred_element_type=F32,
            )
            real_lags = pltpu.roll(gram[:LANES], LANES, 1, stride=1, stride_axis=0)
            imag_lags = pltpu.roll(gram[LANES:], LANES + LAGS, 1, stride=1, stride_axis=0)
            lags = jnp.where(real_lane, real_lags[:, :LANES], imag_lags[:, :LANES])
            high = lags.astype(BF16)
            low = (lags - high.astype(F32)).astype(BF16)
            top = 2 * block * LANES
            lag_ref[top : top + LANES, held] = high
            lag_ref[top + LANES : top + 2 * LANES, held] = low
    gates = [gate_ref[:, b * LANES : (b + 1) * LANES] for b in range(BLOCKS)]
    gates = jnp.concatenate([gate for gate in gates for _ in range(2)], 1)
    sums = jnp.dot(gates, lag_ref[...], preferred_element_type=F32)
    for slot in range(slots):
        sum_ref[slot] = sums[:, slot * LANES : (slot + 1) * LANES] * scale
    for step, out_ref in enumerate(reversed(out_refs)):
        gates = out_ref.shape[1] * out_ref.shape[2]
        first = pl.multiple_of((chip ^ step) * gates, gates)
        out_ref[...] = sum_ref[:, pl.ds(first, gates), :].reshape(out_ref.shape).astype(BF16)


def lag_profiles(place, signs, gate_hot, pieces, sources, slots, scale):
    chips = sources // 2
    row_groups, rows, _ = signs.shape
    out = jax.ShapeDtypeStruct((slots, 2, GATES // sources, LANES), BF16)
    vmem = pl.BlockSpec(memory_space=pltpu.VMEM)
    return pl.pallas_call(
        functools.partial(lag_kernel, scale, len(pieces)),
        in_specs=[pl.BlockSpec(memory_space=pltpu.SMEM)] * 2 + [vmem] * (2 + len(pieces)),
        out_specs=[vmem] * chips,
        out_shape=[out] * chips,
        scratch_shapes=[
            pltpu.VMEM((sources, 2, slots, rows, LANES), BF16),
            pltpu.VMEM((slots, 2 * row_groups * rows, (BLOCKS + 1) * LANES), BF16),
            pltpu.VMEM((2 * IPP_LEN, slots * LANES), BF16),
            pltpu.VMEM((slots, GATES, LANES), F32),
        ],
        compiler_params=pltpu.CompilerParams(vmem_limit_bytes=VMEM),
        name="lag_profiles",
    )(*place, signs, gate_hot, *pieces)


def gather_kernel(width, chip_ref, core_ref, *refs):
    pieces_in = refs[:-1]
    out_ref = refs[-1]
    chips = len(pieces_in) // 2
    beams = out_ref.shape[0]
    slots = pieces_in[0].shape[0]
    chip = chip_ref[0]
    core = core_ref[0]
    for index, ref in enumerate(pieces_in):
        first = (chip ^ (index // 2)) * (beams - width) // (chips - 1)
        first += (core ^ (index % 2)) * (width - slots)
        out_ref[pl.ds(first, slots)] = ref[:, core].astype(F32)


def gather_beams(place, pieces, width, beams):
    gates = pieces[0].shape[2]
    vmem = pl.BlockSpec(memory_space=pltpu.VMEM)
    return pl.pallas_call(
        functools.partial(gather_kernel, width),
        in_specs=[pl.BlockSpec(memory_space=pltpu.SMEM)] * 2 + [vmem] * len(pieces),
        out_specs=vmem,
        out_shape=jax.ShapeDtypeStruct((beams, gates, LANES), F32),
        compiler_params=pltpu.CompilerParams(vmem_limit_bytes=VMEM),
        name="gather_beams",
    )(*place, *pieces)


def sign_rows(code_signs, periods, row_groups):
    signs = jnp.repeat((2 * code_signs - 1).astype(F32), BAUD_LEN, axis=1)
    signs = jnp.tile(signs, (periods // NCODES, 1))
    return signs.reshape(periods // row_groups, row_groups, LANES).transpose(1, 0, 2)


def gate_rows(gate_map):
    position = jnp.arange(IPP_LEN)
    position = position // LANES * LANES + (LANES - 1 - position % LANES)
    gates = jnp.repeat(gate_map, SEC_LEN).reshape(BLOCKS, LANES)[:, ::-1].reshape(IPP_LEN)
    return (jnp.arange(GATES)[:, None] == gates[None, :]).astype(BF16)


def exchanged(block, axis, step):
    return lax.ppermute(block, axis, [(i, i ^ step) for i in range(lax.axis_size(axis))])


def spread(blocks):
    pieces = []
    for step, block in enumerate(blocks):
        block = exchanged(block, "tm", 2 * step) if step else block
        pieces += [block, exchanged(block, "tm", 1)]
    return pieces


def body(streams, beam_weights, code_signs, gate_map):
    groups = lax.axis_size("sub")
    sources = lax.axis_size("tm")
    chips = sources // 2
    beams = beam_weights.shape[1] // groups
    samples = streams.shape[2]
    width = -(-beams // chips)
    slots = -(-width // 2)
    periods = samples * sources // IPP_LEN
    scale = 1.0 / math.sqrt(periods * IPP_LEN / GATES)
    here = lax.axis_index("sub")
    chip = lax.axis_index("tm") // 2
    place = (chip.reshape(1), (lax.axis_index("tm") % 2).reshape(1))
    signs = sign_rows(code_signs, periods, sources // PER_ROW)
    gate_hot = gate_rows(gate_map)
    weights = pltpu.with_memory_space_constraint(beam_weights.transpose(1, 0, 2), pltpu.HBM)
    limit = 2 * streams.shape[1] * STREAM_MAX * WEIGHT_MAX
    gain = 2.0 ** math.floor(math.log2(60000.0 / limit))
    by_channel = streams.transpose(1, 0, 2)

    def first_of(owner):
        return owner * (beams - width) // (chips - 1)

    half = chips // 2
    count = max((half - 1) * (beams - width) // (chips - 1) + width, beams - first_of(half))
    low = chip < half
    blocks = [None] * chips
    for far in (True, False):
        start = jnp.where(low == far, beams - count, 0).astype(jnp.int32)
        partial = partial_beams(by_channel, weights, here, start, groups, count)
        total = partial[0]
        for step in range(groups - 1, 0, -1):
            came = exchanged((partial[step] * gain).astype(jnp.float16), "sub", step)
            total = total + came.astype(F32) * (1.0 / gain)
        total = total.astype(BF16)
        for step in range(half, chips) if far else range(half):
            place_of = first_of(chip ^ step) - start
            blocks[step] = lax.dynamic_slice_in_dim(total, place_of, width, 1)
    terms = lag_profiles(place, signs, gate_hot, spread(blocks), sources, slots, scale)
    return gather_beams(place, spread(terms[::-1]), width, beams).transpose(1, 0, 2)


def solution(mesh):
    placed = (P(None, "sub", "tm"), P(None, None, "sub"), P(), P())
    return jax.shard_map(
        body, mesh=mesh, in_specs=placed, out_specs=P("tm", "sub", None), check_vma=False
    )
```

```python
import functools
import math

import jax
import jax.numpy as jnp
from jax import lax
from jax.experimental import pallas as pl
from jax.experimental.pallas import tpu as pltpu
from jax.sharding import PartitionSpec as P

PKT = 32
IPP_LEN = 512
LAGS = 64
NCODES = 32
BAUD_LEN = 8
SEC_LEN = 2
GATES = 128
LANES = 128
BLOCKS = IPP_LEN // LANES
PER_ROW = LANES // PKT
PKTS = IPP_LEN // PKT
STREAM_MAX = 6.0
WEIGHT_MAX = 0.09375
VMEM = 48 * 1024 * 1024
SLICE = 8
F32 = jnp.float32
BF16 = jnp.bfloat16


def beam_kernel(here_ref, start_ref, w_hbm, x_hbm, *refs):
    out_refs = refs[:-6]
    w_ref, x_ref, first_ref, second_ref, mixed_ref, sems = refs[-6:]
    groups = len(out_refs)
    depth = w_ref.shape[2]
    slices, _, _, width = x_ref.shape
    half = mixed_ref.shape[0] // 2
    count = out_refs[0].shape[1]
    w_copy = pltpu.make_async_copy(w_hbm, w_ref, sems.at[slices])
    w_copy.start()
    copies = []
    for index in range(slices):
        columns = pl.ds(index * width, width)
        copies.append(
            pltpu.make_async_copy(x_hbm.at[:, :, columns], x_ref.at[index], sems.at[index])
        )
        copies[-1].start()
    first_ref[...] = jnp.zeros_like(first_ref)
    second_ref[...] = jnp.zeros_like(second_ref)
    source = lax.broadcasted_iota(jnp.int32, (2 * LANES, 2 * LANES), 0)
    target = lax.broadcasted_iota(jnp.int32, (2 * LANES, 2 * LANES), 1)
    weave = source % LANES * 2 + source // LANES == target
    weave = weave.astype(F32).astype(BF16)
    w_copy.wait()
    for group in range(groups):
        owner = here_ref[0] ^ group
        chosen = pl.ds(owner * (w_ref.shape[0] // groups) + start_ref[0], count)
        weights = w_ref[chosen].astype(F32)
        real = weights[:, 0, :]
        imag = weights[:, 1, :]
        top = group * count
        first_ref[top : top + count, :depth] = real
        first_ref[half + top : half + top + count, :depth] = imag
        second_ref[top : top + count, :depth] = -imag
        second_ref[half + top : half + top + count, :depth] = real
    for block in range(first_ref.shape[1] // LANES):
        columns = slice(block * LANES, (block + 1) * LANES)
        pair = jnp.concatenate([first_ref[:, columns], second_ref[:, columns]], 1)
        woven = jnp.dot(pair.astype(BF16), weave, preferred_element_type=F32)
        mixed_ref[:, 2 * block * LANES : 2 * (block + 1) * LANES] = woven.astype(BF16)
    for index in range(slices):
        copies[index].wait()
        product = jnp.dot(
            mixed_ref[:, : 2 * depth],
            x_ref[index].reshape(2 * depth, width),
            preferred_element_type=F32,
        )
        rows = product.reshape(2 * half, width // LANES, LANES)
        place = slice(index * (width // LANES), (index + 1) * (width // LANES))
        for group, out_ref in enumerate(out_refs):
            top = group * count
            out_ref[0, :, place, :] = rows[top : top + count]
            out_ref[1, :, place, :] = rows[half + top : half + top + count]


def partial_beams(streams, weights, here, start, groups, count):
    depth, _, samples = streams.shape
    beams = groups * count
    width = SLICE * LANES
    rows = 2 * (-(-beams // 8) * 8)
    columns = -(-depth // LANES) * LANES
    return pl.pallas_call(
        beam_kernel,
        in_specs=[pl.BlockSpec(memory_space=pltpu.SMEM)] * 2
        + [pl.BlockSpec(memory_space=pltpu.HBM)] * 2,
        out_specs=[pl.BlockSpec(memory_space=pltpu.VMEM)] * groups,
        out_shape=[jax.ShapeDtypeStruct((2, count, samples // LANES, LANES), F32)] * groups,
        scratch_shapes=[
            pltpu.VMEM(weights.shape, BF16),
            pltpu.VMEM((samples // width, depth, 2, width), BF16),
            pltpu.VMEM((rows, columns), F32),
            pltpu.VMEM((rows, columns), F32),
            pltpu.VMEM((rows, 2 * columns), BF16),
            pltpu.SemaphoreType.DMA((samples // width + 1,)),
        ],
        compiler_params=pltpu.CompilerParams(vmem_limit_bytes=VMEM),
        cost_estimate=pl.CostEstimate(
            flops=8 * beams * depth * samples,
            bytes_accessed=4 * depth * samples + 8 * beams * samples,
            transcendentals=0,
        ),
        name="partial_beams",
    )(here.reshape(1), start.reshape(1), weights, streams)


def lag_kernel(scale, count, chip_ref, core_ref, sign_ref, gate_ref, *refs):
    pieces_in = refs[:count]
    out_refs = refs[count:-4]
    x_ref, both_ref, lag_ref, sum_ref = refs[-4:]
    sources, _, slots, rows, _ = x_ref.shape
    chip = chip_ref[0]
    core = core_ref[0]
    taken = pieces_in[0].shape[1] - slots
    for index, ref in enumerate(pieces_in):
        source = 2 * (chip ^ (index // 2)) + (core ^ (index % 2))
        x_ref[source] = ref[:, pl.ds(core * taken, slots)]
    row_groups = sign_ref.shape[0]
    depth = row_groups * rows
    lane = lax.broadcasted_iota(jnp.int32, (rows, LANES), 1)
    row = lax.broadcasted_iota(jnp.int32, (rows, LANES), 0)
    flip = (
        lax.broadcasted_iota(jnp.int32, (LANES, LANES), 0)
        + lax.broadcasted_iota(jnp.int32, (LANES, LANES), 1)
        == LANES - 1
    ).astype(F32).astype(BF16)
    real_lane = lax.broadcasted_iota(jnp.int32, (LANES, LANES), 1) < LAGS
    real_depth = lax.broadcasted_iota(jnp.int32, (LANES, 2 * depth), 1) < depth

    def assemble(slot, part):
        loaded = [x_ref[d, part, slot].astype(F32) for d in range(sources)]
        raw = []
        for group in range(row_groups):
            blocks = []
            for block in range(BLOCKS):
                total = None
                for place in range(PER_ROW):
                    packet = group * PKTS + block * PER_ROW + place
                    shift = (place - packet // sources) * PKT % LANES
                    piece = loaded[packet % sources]
                    if shift:
                        piece = pltpu.roll(piece, shift, 1)
                    total = piece if total is None else jnp.where(lane >= place * PKT, piece, total)
                blocks.append(total)
            raw.append(blocks)
        raw.append([jnp.where(row == rows - 1, 0.0, pltpu.roll(raw[0][0], rows - 1, 0))])
        for group in range(row_groups):
            top = part * depth + group * rows
            for block in range(BLOCKS + 1):
                piece = raw[group][block] if block < BLOCKS else raw[group + 1][0]
                columns = slice(block * LANES, (block + 1) * LANES)
                both_ref[slot, top : top + rows, columns] = (piece * sign_ref[group]).astype(BF16)

    for slot in range(slots):
        assemble(slot, 0)
        assemble(slot, 1)
    for slot in range(slots):
        held = slice(slot * LANES, (slot + 1) * LANES)
        for block in range(BLOCKS):
            columns = slice(block * LANES, (block + 1) * LANES)
            base = lax.dot_general(
                flip,
                both_ref[slot, :, columns],
                (((1,), (1,)), ((), ())),
                preferred_element_type=F32,
            )
            swapped = pltpu.roll(base, depth, 1)
            turned = jnp.where(real_depth, -swapped, swapped)
            gram = jnp.dot(
                jnp.concatenate([base, turned], 0).astype(BF16),
                both_ref[slot, :, block * LANES : (block + 2) * LANES],
                preferred_element_type=F32,
            )
            real_lags = pltpu.roll(gram[:LANES], LANES, 1, stride=1, stride_axis=0)
            imag_lags = pltpu.roll(gram[LANES:], LANES + LAGS, 1, stride=1, stride_axis=0)
            lags = jnp.where(real_lane, real_lags[:, :LANES], imag_lags[:, :LANES])
            high = lags.astype(BF16)
            low = (lags - high.astype(F32)).astype(BF16)
            top = 2 * block * LANES
            lag_ref[top : top + LANES, held] = high
            lag_ref[top + LANES : top + 2 * LANES, held] = low
    gates = [gate_ref[:, b * LANES : (b + 1) * LANES] for b in range(BLOCKS)]
    gates = jnp.concatenate([gate for gate in gates for _ in range(2)], 1)
    sums = jnp.dot(gates, lag_ref[...], preferred_element_type=F32)
    for slot in range(slots):
        sum_ref[slot] = sums[:, slot * LANES : (slot + 1) * LANES] * scale
    for step, out_ref in enumerate(reversed(out_refs)):
        gates = out_ref.shape[1] * out_ref.shape[2]
        first = pl.multiple_of((chip ^ step) * gates, gates)
        out_ref[...] = sum_ref[:, pl.ds(first, gates), :].reshape(out_ref.shape).astype(BF16)


def lag_profiles(place, signs, gate_hot, pieces, sources, slots, scale):
    chips = sources // 2
    row_groups, rows, _ = signs.shape
    out = jax.ShapeDtypeStruct((slots, 2, GATES // sources, LANES), BF16)
    vmem = pl.BlockSpec(memory_space=pltpu.VMEM)
    return pl.pallas_call(
        functools.partial(lag_kernel, scale, len(pieces)),
        in_specs=[pl.BlockSpec(memory_space=pltpu.SMEM)] * 2 + [vmem] * (2 + len(pieces)),
        out_specs=[vmem] * chips,
        out_shape=[out] * chips,
        scratch_shapes=[
            pltpu.VMEM((sources, 2, slots, rows, LANES), BF16),
            pltpu.VMEM((slots, 2 * row_groups * rows, (BLOCKS + 1) * LANES), BF16),
            pltpu.VMEM((2 * IPP_LEN, slots * LANES), BF16),
            pltpu.VMEM((slots, GATES, LANES), F32),
        ],
        compiler_params=pltpu.CompilerParams(vmem_limit_bytes=VMEM),
        name="lag_profiles",
    )(*place, signs, gate_hot, *pieces)


def gather_kernel(width, chip_ref, core_ref, *refs):
    pieces_in = refs[:-1]
    out_ref = refs[-1]
    chips = len(pieces_in) // 2
    beams = out_ref.shape[0]
    slots = pieces_in[0].shape[0]
    chip = chip_ref[0]
    core = core_ref[0]
    for index, ref in enumerate(reversed(pieces_in)):
        first = (chip ^ (index // 2)) * (beams - width) // (chips - 1)
        first += (core ^ (index % 2)) * (width - slots)
        out_ref[pl.ds(first, slots)] = ref[:, core].astype(F32)


def gather_beams(place, pieces, width, beams):
    gates = pieces[0].shape[2]
    vmem = pl.BlockSpec(memory_space=pltpu.VMEM)
    return pl.pallas_call(
        functools.partial(gather_kernel, width),
        in_specs=[pl.BlockSpec(memory_space=pltpu.SMEM)] * 2 + [vmem] * len(pieces),
        out_specs=vmem,
        out_shape=jax.ShapeDtypeStruct((beams, gates, LANES), F32),
        compiler_params=pltpu.CompilerParams(vmem_limit_bytes=VMEM),
        name="gather_beams",
    )(*place, *reversed(pieces))


def sign_rows(code_signs, periods, row_groups):
    signs = jnp.repeat((2 * code_signs - 1).astype(F32), BAUD_LEN, axis=1)
    signs = jnp.tile(signs, (periods // NCODES, 1))
    return signs.reshape(periods // row_groups, row_groups, LANES).transpose(1, 0, 2)


def gate_rows(gate_map):
    position = jnp.arange(IPP_LEN)
    position = position // LANES * LANES + (LANES - 1 - position % LANES)
    gates = jnp.repeat(gate_map, SEC_LEN).reshape(BLOCKS, LANES)[:, ::-1].reshape(IPP_LEN)
    return (jnp.arange(GATES)[:, None] == gates[None, :]).astype(BF16)


def exchanged(block, axis, step):
    return lax.ppermute(block, axis, [(i, i ^ step) for i in range(lax.axis_size(axis))])


def spread(blocks):
    pieces = []
    for step, block in enumerate(blocks):
        block = exchanged(block, "tm", 2 * step) if step else block
        pieces += [block, exchanged(block, "tm", 1)]
    return pieces


def body(streams, beam_weights, code_signs, gate_map):
    groups = lax.axis_size("sub")
    sources = lax.axis_size("tm")
    chips = sources // 2
    beams = beam_weights.shape[1] // groups
    samples = streams.shape[2]
    width = -(-beams // chips)
    slots = -(-width // 2)
    periods = samples * sources // IPP_LEN
    scale = 1.0 / math.sqrt(periods * IPP_LEN / GATES)
    here = lax.axis_index("sub")
    chip = lax.axis_index("tm") // 2
    place = (chip.reshape(1), (lax.axis_index("tm") % 2).reshape(1))
    signs = sign_rows(code_signs, periods, sources // PER_ROW)
    gate_hot = gate_rows(gate_map)
    weights = pltpu.with_memory_space_constraint(beam_weights.transpose(1, 0, 2), pltpu.HBM)
    limit = 2 * streams.shape[1] * STREAM_MAX * WEIGHT_MAX
    gain = 2.0 ** math.floor(math.log2(60000.0 / limit))
    by_channel = streams.transpose(1, 0, 2)

    def first_of(owner):
        return owner * (beams - width) // (chips - 1)

    half = chips // 2
    count = max((half - 1) * (beams - width) // (chips - 1) + width, beams - first_of(half))
    low = chip < half
    blocks = [None] * chips
    for far in (True, False):
        start = jnp.where(low == far, beams - count, 0).astype(jnp.int32)
        partial = partial_beams(by_channel, weights, here, start, groups, count)
        total = partial[0]
        for step in range(groups - 1, 0, -1):
            came = exchanged((partial[step] * gain).astype(jnp.float16), "sub", step)
            total = total + came.astype(F32) * (1.0 / gain)
        total = total.astype(BF16)
        for step in range(half, chips) if far else range(half):
            place_of = first_of(chip ^ step) - start
            blocks[step] = lax.dynamic_slice_in_dim(total, place_of, width, 1)
    terms = lag_profiles(place, signs, gate_hot, spread(blocks), sources, slots, scale)
    return gather_beams(place, spread(terms[::-1]), width, beams).transpose(1, 0, 2)


def solution(mesh):
    placed = (P(None, "sub", "tm"), P(None, None, "sub"), P(), P())
    return jax.shard_map(
        body, mesh=mesh, in_specs=placed, out_specs=P("tm", "sub", None), check_vma=False
    )
```

```python
import functools
import math

import jax
import jax.numpy as jnp
from jax import lax
from jax.experimental import pallas as pl
from jax.experimental.pallas import tpu as pltpu
from jax.sharding import PartitionSpec as P

PKT = 32
IPP_LEN = 512
LAGS = 64
NCODES = 32
BAUD_LEN = 8
SEC_LEN = 2
GATES = 128
LANES = 128
BLOCKS = IPP_LEN // LANES
PER_ROW = LANES // PKT
PKTS = IPP_LEN // PKT
STREAM_MAX = 6.0
WEIGHT_MAX = 0.09375
VMEM = 48 * 1024 * 1024
SLICE = 8
F32 = jnp.float32
BF16 = jnp.bfloat16


def beam_kernel(here_ref, start_ref, w_hbm, x_hbm, *refs):
    out_refs = refs[:-6]
    w_ref, x_ref, first_ref, second_ref, mixed_ref, sems = refs[-6:]
    groups = len(out_refs)
    depth = w_ref.shape[2]
    slices, _, _, width = x_ref.shape
    half = mixed_ref.shape[0] // 2
    count = out_refs[0].shape[1]
    w_copy = pltpu.make_async_copy(w_hbm, w_ref, sems.at[slices])
    w_copy.start()
    copies = []
    for index in range(slices):
        columns = pl.ds(index * width, width)
        copies.append(
            pltpu.make_async_copy(x_hbm.at[:, :, columns], x_ref.at[index], sems.at[index])
        )
        copies[-1].start()
    first_ref[...] = jnp.zeros_like(first_ref)
    second_ref[...] = jnp.zeros_like(second_ref)
    source = lax.broadcasted_iota(jnp.int32, (2 * LANES, 2 * LANES), 0)
    target = lax.broadcasted_iota(jnp.int32, (2 * LANES, 2 * LANES), 1)
    weave = source % LANES * 2 + source // LANES == target
    weave = weave.astype(F32).astype(BF16)
    w_copy.wait()
    for group in range(groups):
        owner = here_ref[0] ^ group
        chosen = pl.ds(owner * (w_ref.shape[0] // groups) + start_ref[0], count)
        weights = w_ref[chosen].astype(F32)
        real = weights[:, 0, :]
        imag = weights[:, 1, :]
        top = group * count
        first_ref[top : top + count, :depth] = real
        first_ref[half + top : half + top + count, :depth] = imag
        second_ref[top : top + count, :depth] = -imag
        second_ref[half + top : half + top + count, :depth] = real
    for block in range(first_ref.shape[1] // LANES):
        columns = slice(block * LANES, (block + 1) * LANES)
        pair = jnp.concatenate([first_ref[:, columns], second_ref[:, columns]], 1)
        woven = jnp.dot(pair.astype(BF16), weave, preferred_element_type=F32)
        mixed_ref[:, 2 * block * LANES : 2 * (block + 1) * LANES] = woven.astype(BF16)
    for index in range(slices):
        copies[index].wait()
        product = jnp.dot(
            mixed_ref[:, : 2 * depth],
            x_ref[index].reshape(2 * depth, width),
            preferred_element_type=F32,
        )
        rows = product.reshape(2 * half, width // LANES, LANES)
        place = slice(index * (width // LANES), (index + 1) * (width // LANES))
        for group, out_ref in enumerate(out_refs):
            top = group * count
            out_ref[0, :, place, :] = rows[top : top + count]
            out_ref[1, :, place, :] = rows[half + top : half + top + count]


def partial_beams(streams, weights, here, start, groups, count):
    depth, _, samples = streams.shape
    beams = groups * count
    width = SLICE * LANES
    rows = 2 * (-(-beams // 8) * 8)
    columns = -(-depth // LANES) * LANES
    return pl.pallas_call(
        beam_kernel,
        in_specs=[pl.BlockSpec(memory_space=pltpu.SMEM)] * 2
        + [pl.BlockSpec(memory_space=pltpu.HBM)] * 2,
        out_specs=[pl.BlockSpec(memory_space=pltpu.VMEM)] * groups,
        out_shape=[jax.ShapeDtypeStruct((2, count, samples // LANES, LANES), F32)] * groups,
        scratch_shapes=[
            pltpu.VMEM(weights.shape, BF16),
            pltpu.VMEM((samples // width, depth, 2, width), BF16),
            pltpu.VMEM((rows, columns), F32),
            pltpu.VMEM((rows, columns), F32),
            pltpu.VMEM((rows, 2 * columns), BF16),
            pltpu.SemaphoreType.DMA((samples // width + 1,)),
        ],
        compiler_params=pltpu.CompilerParams(vmem_limit_bytes=VMEM),
        cost_estimate=pl.CostEstimate(
            flops=8 * beams * depth * samples,
            bytes_accessed=4 * depth * samples + 8 * beams * samples,
            transcendentals=0,
        ),
        name="partial_beams",
    )(here.reshape(1), start.reshape(1), weights, streams)


def lag_kernel(scale, count, chip_ref, core_ref, sign_ref, gate_ref, *refs):
    pieces_in = refs[:count]
    out_refs = refs[count:-4]
    x_ref, both_ref, lag_ref, sum_ref = refs[-4:]
    sources, _, slots, rows, _ = x_ref.shape
    chip = chip_ref[0]
    core = core_ref[0]
    taken = pieces_in[0].shape[1] - slots
    for index, ref in enumerate(pieces_in):
        source = 2 * (chip ^ (index // 2)) + (core ^ (index % 2))
        if ref.shape[1] == slots:
            x_ref[source] = ref[...]
        else:
            x_ref[source] = ref[:, pl.ds(core * taken, slots)]
    row_groups = sign_ref.shape[0]
    depth = row_groups * rows
    lane = lax.broadcasted_iota(jnp.int32, (rows, LANES), 1)
    row = lax.broadcasted_iota(jnp.int32, (rows, LANES), 0)
    flip = (
        lax.broadcasted_iota(jnp.int32, (LANES, LANES), 0)
        + lax.broadcasted_iota(jnp.int32, (LANES, LANES), 1)
        == LANES - 1
    ).astype(F32).astype(BF16)
    real_lane = lax.broadcasted_iota(jnp.int32, (LANES, LANES), 1) < LAGS
    real_depth = lax.broadcasted_iota(jnp.int32, (LANES, 2 * depth), 1) < depth

    def assemble(slot, part):
        loaded = [x_ref[d, part, slot].astype(F32) for d in range(sources)]
        raw = []
        for group in range(row_groups):
            blocks = []
            for block in range(BLOCKS):
                total = None
                for place in range(PER_ROW):
                    packet = group * PKTS + block * PER_ROW + place
                    shift = (place - packet // sources) * PKT % LANES
                    piece = loaded[packet % sources]
                    if shift:
                        piece = pltpu.roll(piece, shift, 1)
                    total = piece if total is None else jnp.where(lane >= place * PKT, piece, total)
                blocks.append(total)
            raw.append(blocks)
        raw.append([jnp.where(row == rows - 1, 0.0, pltpu.roll(raw[0][0], rows - 1, 0))])
        for group in range(row_groups):
            top = part * depth + group * rows
            for block in range(BLOCKS + 1):
                piece = raw[group][block] if block < BLOCKS else raw[group + 1][0]
                columns = slice(block * LANES, (block + 1) * LANES)
                both_ref[slot, top : top + rows, columns] = (piece * sign_ref[group]).astype(BF16)

    for slot in range(slots):
        assemble(slot, 0)
        assemble(slot, 1)
    for slot in range(slots):
        held = slice(slot * LANES, (slot + 1) * LANES)
        for block in range(BLOCKS):
            columns = slice(block * LANES, (block + 1) * LANES)
            base = lax.dot_general(
                flip,
                both_ref[slot, :, columns],
                (((1,), (1,)), ((), ())),
                preferred_element_type=F32,
            )
            swapped = pltpu.roll(base, depth, 1)
            turned = jnp.where(real_depth, -swapped, swapped)
            gram = jnp.dot(
                jnp.concatenate([base, turned], 0).astype(BF16),
                both_ref[slot, :, block * LANES : (block + 2) * LANES],
                preferred_element_type=F32,
            )
            real_lags = pltpu.roll(gram[:LANES], LANES, 1, stride=1, stride_axis=0)
            imag_lags = pltpu.roll(gram[LANES:], LANES + LAGS, 1, stride=1, stride_axis=0)
            lags = jnp.where(real_lane, real_lags[:, :LANES], imag_lags[:, :LANES])
            high = lags.astype(BF16)
            low = (lags - high.astype(F32)).astype(BF16)
            top = 2 * block * LANES
            lag_ref[top : top + LANES, held] = high
            lag_ref[top + LANES : top + 2 * LANES, held] = low
    gates = [gate_ref[:, b * LANES : (b + 1) * LANES] for b in range(BLOCKS)]
    gates = jnp.concatenate([gate for gate in gates for _ in range(2)], 1)
    sums = jnp.dot(gates, lag_ref[...], preferred_element_type=F32)
    for slot in range(slots):
        sum_ref[slot] = sums[:, slot * LANES : (slot + 1) * LANES] * scale
    for step, out_ref in enumerate(reversed(out_refs)):
        gates = out_ref.shape[1] * out_ref.shape[2]
        first = pl.multiple_of((chip ^ step) * gates, gates)
        out_ref[...] = sum_ref[:, pl.ds(first, gates), :].reshape(out_ref.shape).astype(BF16)


def lag_profiles(place, signs, gate_hot, pieces, sources, slots, scale):
    chips = sources // 2
    row_groups, rows, _ = signs.shape
    out = jax.ShapeDtypeStruct((slots, 2, GATES // sources, LANES), BF16)
    vmem = pl.BlockSpec(memory_space=pltpu.VMEM)
    return pl.pallas_call(
        functools.partial(lag_kernel, scale, len(pieces)),
        in_specs=[pl.BlockSpec(memory_space=pltpu.SMEM)] * 2 + [vmem] * (2 + len(pieces)),
        out_specs=[vmem] * chips,
        out_shape=[out] * chips,
        scratch_shapes=[
            pltpu.VMEM((sources, 2, slots, rows, LANES), BF16),
            pltpu.VMEM((slots, 2 * row_groups * rows, (BLOCKS + 1) * LANES), BF16),
            pltpu.VMEM((2 * IPP_LEN, slots * LANES), BF16),
            pltpu.VMEM((slots, GATES, LANES), F32),
        ],
        compiler_params=pltpu.CompilerParams(vmem_limit_bytes=VMEM),
        name="lag_profiles",
    )(*place, signs, gate_hot, *pieces)


def gather_kernel(width, chip_ref, core_ref, *refs):
    pieces_in = refs[:-1]
    out_ref = refs[-1]
    chips = len(pieces_in) // 2
    beams = out_ref.shape[0]
    slots = pieces_in[0].shape[0]
    chip = chip_ref[0]
    core = core_ref[0]
    for index, ref in enumerate(reversed(pieces_in)):
        first = (chip ^ (index // 2)) * (beams - width) // (chips - 1)
        first += (core ^ (index % 2)) * (width - slots)
        out_ref[pl.ds(first, slots)] = ref[:, core].astype(F32)


def gather_beams(place, pieces, width, beams):
    gates = pieces[0].shape[2]
    vmem = pl.BlockSpec(memory_space=pltpu.VMEM)
    return pl.pallas_call(
        functools.partial(gather_kernel, width),
        in_specs=[pl.BlockSpec(memory_space=pltpu.SMEM)] * 2 + [vmem] * len(pieces),
        out_specs=vmem,
        out_shape=jax.ShapeDtypeStruct((beams, gates, LANES), F32),
        compiler_params=pltpu.CompilerParams(vmem_limit_bytes=VMEM),
        name="gather_beams",
    )(*place, *reversed(pieces))


def sign_rows(code_signs, periods, row_groups):
    signs = jnp.repeat((2 * code_signs - 1).astype(F32), BAUD_LEN, axis=1)
    signs = jnp.tile(signs, (periods // NCODES, 1))
    return signs.reshape(periods // row_groups, row_groups, LANES).transpose(1, 0, 2)


def gate_rows(gate_map):
    position = jnp.arange(IPP_LEN)
    position = position // LANES * LANES + (LANES - 1 - position % LANES)
    gates = jnp.repeat(gate_map, SEC_LEN).reshape(BLOCKS, LANES)[:, ::-1].reshape(IPP_LEN)
    return (jnp.arange(GATES)[:, None] == gates[None, :]).astype(BF16)


def exchanged(block, axis, step):
    return lax.ppermute(block, axis, [(i, i ^ step) for i in range(lax.axis_size(axis))])


def spread(blocks):
    pieces = []
    for step, block in enumerate(blocks):
        block = exchanged(block, "tm", 2 * step) if step else block
        pieces += [block, exchanged(block, "tm", 1)]
    return pieces


def body(streams, beam_weights, code_signs, gate_map):
    groups = lax.axis_size("sub")
    sources = lax.axis_size("tm")
    chips = sources // 2
    beams = beam_weights.shape[1] // groups
    samples = streams.shape[2]
    width = -(-beams // chips)
    slots = -(-width // 2)
    periods = samples * sources // IPP_LEN
    scale = 1.0 / math.sqrt(periods * IPP_LEN / GATES)
    here = lax.axis_index("sub")
    chip = lax.axis_index("tm") // 2
    core = lax.axis_index("tm") % 2
    place = (chip.reshape(1), core.reshape(1))
    signs = sign_rows(code_signs, periods, sources // PER_ROW)
    gate_hot = gate_rows(gate_map)
    weights = pltpu.with_memory_space_constraint(beam_weights.transpose(1, 0, 2), pltpu.HBM)
    limit = 2 * streams.shape[1] * STREAM_MAX * WEIGHT_MAX
    gain = 2.0 ** math.floor(math.log2(60000.0 / limit))
    by_channel = streams.transpose(1, 0, 2)

    def first_of(owner):
        return owner * (beams - width) // (chips - 1)

    half = chips // 2
    count = max((half - 1) * (beams - width) // (chips - 1) + width, beams - first_of(half))
    low = chip < half
    pieces = [None] * sources
    for far in (True, False):
        start = jnp.where(low == far, beams - count, 0).astype(jnp.int32)
        partial = partial_beams(by_channel, weights, here, start, groups, count)
        total = partial[0]
        for step in range(groups - 1, 0, -1):
            came = exchanged((partial[step] * gain).astype(jnp.float16), "sub", step)
            total = total + came.astype(F32) * (1.0 / gain)
        total = total.astype(BF16)
        for step in range(half, chips) if far else range(half):
            place_of = first_of(chip ^ step) - start
            if far or not step:
                block = lax.dynamic_slice_in_dim(total, place_of, width, 1)
                block = exchanged(block, "tm", 2 * step) if step else block
                pieces[2 * step : 2 * step + 2] = [block, exchanged(block, "tm", 1)]
            else:
                for other in range(2):
                    first = place_of + (core ^ other) * (width - slots)
                    block = lax.dynamic_slice_in_dim(total, first, slots, 1)
                    pieces[2 * step + other] = exchanged(block, "tm", 2 * step + other)
    terms = lag_profiles(place, signs, gate_hot, pieces, sources, slots, scale)
    return gather_beams(place, spread(terms[::-1]), width, beams).transpose(1, 0, 2)


def solution(mesh):
    placed = (P(None, "sub", "tm"), P(None, None, "sub"), P(), P())
    return jax.shard_map(
        body, mesh=mesh, in_specs=placed, out_specs=P("tm", "sub", None), check_vma=False
    )
```

```python
import functools
import math

import jax
import jax.numpy as jnp
from jax import lax
from jax.experimental import pallas as pl
from jax.experimental.pallas import tpu as pltpu
from jax.sharding import PartitionSpec as P

PKT = 32
IPP_LEN = 512
LAGS = 64
NCODES = 32
BAUD_LEN = 8
SEC_LEN = 2
GATES = 128
LANES = 128
BLOCKS = IPP_LEN // LANES
PER_ROW = LANES // PKT
PKTS = IPP_LEN // PKT
STREAM_MAX = 6.0
WEIGHT_MAX = 0.09375
VMEM = 48 * 1024 * 1024
SLICE = 8
F32 = jnp.float32
BF16 = jnp.bfloat16


def beam_kernel(here_ref, start_ref, w_hbm, x_hbm, *refs):
    out_refs = refs[:-6]
    w_ref, x_ref, first_ref, second_ref, mixed_ref, sems = refs[-6:]
    groups = len(out_refs)
    depth = w_ref.shape[2]
    slices, _, _, width = x_ref.shape
    half = mixed_ref.shape[0] // 2
    count = out_refs[0].shape[1]
    w_copy = pltpu.make_async_copy(w_hbm, w_ref, sems.at[slices])
    w_copy.start()
    copies = []
    for index in range(slices):
        columns = pl.ds(index * width, width)
        copies.append(
            pltpu.make_async_copy(x_hbm.at[:, :, columns], x_ref.at[index], sems.at[index])
        )
        copies[-1].start()
    first_ref[...] = jnp.zeros_like(first_ref)
    second_ref[...] = jnp.zeros_like(second_ref)
    source = lax.broadcasted_iota(jnp.int32, (2 * LANES, 2 * LANES), 0)
    target = lax.broadcasted_iota(jnp.int32, (2 * LANES, 2 * LANES), 1)
    weave = source % LANES * 2 + source // LANES == target
    weave = weave.astype(F32).astype(BF16)
    w_copy.wait()
    for group in range(groups):
        owner = here_ref[0] ^ group
        chosen = pl.ds(owner * (w_ref.shape[0] // groups) + start_ref[0], count)
        weights = w_ref[chosen].astype(F32)
        real = weights[:, 0, :]
        imag = weights[:, 1, :]
        top = group * count
        first_ref[top : top + count, :depth] = real
        first_ref[half + top : half + top + count, :depth] = imag
        second_ref[top : top + count, :depth] = -imag
        second_ref[half + top : half + top + count, :depth] = real
    for block in range(first_ref.shape[1] // LANES):
        columns = slice(block * LANES, (block + 1) * LANES)
        pair = jnp.concatenate([first_ref[:, columns], second_ref[:, columns]], 1)
        woven = jnp.dot(pair.astype(BF16), weave, preferred_element_type=F32)
        mixed_ref[:, 2 * block * LANES : 2 * (block + 1) * LANES] = woven.astype(BF16)
    for index in range(slices):
        copies[index].wait()
        product = jnp.dot(
            mixed_ref[:, : 2 * depth],
            x_ref[index].reshape(2 * depth, width),
            preferred_element_type=F32,
        )
        rows = product.reshape(2 * half, width // LANES, LANES)
        place = slice(index * (width // LANES), (index + 1) * (width // LANES))
        for group, out_ref in enumerate(out_refs):
            top = group * count
            out_ref[0, :, place, :] = rows[top : top + count]
            out_ref[1, :, place, :] = rows[half + top : half + top + count]


def partial_beams(streams, weights, here, start, groups, count):
    depth, _, samples = streams.shape
    beams = groups * count
    width = SLICE * LANES
    rows = 2 * (-(-beams // 8) * 8)
    columns = -(-depth // LANES) * LANES
    return pl.pallas_call(
        beam_kernel,
        in_specs=[pl.BlockSpec(memory_space=pltpu.SMEM)] * 2
        + [pl.BlockSpec(memory_space=pltpu.HBM)] * 2,
        out_specs=[pl.BlockSpec(memory_space=pltpu.VMEM)] * groups,
        out_shape=[jax.ShapeDtypeStruct((2, count, samples // LANES, LANES), F32)] * groups,
        scratch_shapes=[
            pltpu.VMEM(weights.shape, BF16),
            pltpu.VMEM((samples // width, depth, 2, width), BF16),
            pltpu.VMEM((rows, columns), F32),
            pltpu.VMEM((rows, columns), F32),
            pltpu.VMEM((rows, 2 * columns), BF16),
            pltpu.SemaphoreType.DMA((samples // width + 1,)),
        ],
        compiler_params=pltpu.CompilerParams(vmem_limit_bytes=VMEM),
        cost_estimate=pl.CostEstimate(
            flops=8 * beams * depth * samples,
            bytes_accessed=4 * depth * samples + 8 * beams * samples,
            transcendentals=0,
        ),
        name="partial_beams",
    )(here.reshape(1), start.reshape(1), weights, streams)


def lag_kernel(scale, count, chip_ref, core_ref, sign_ref, gate_ref, *refs):
    pieces_in = refs[:count]
    out_refs = refs[count:-5]
    x_ref, both_ref, back_ref, lag_ref, sum_ref = refs[-5:]
    sources, _, slots, rows, _ = x_ref.shape
    chip = chip_ref[0]
    core = core_ref[0]
    taken = pieces_in[0].shape[1] - slots
    for index, ref in enumerate(pieces_in):
        source = 2 * (chip ^ (index // 2)) + (core ^ (index % 2))
        if ref.shape[1] == slots:
            x_ref[source] = ref[...]
        else:
            x_ref[source] = ref[:, pl.ds(core * taken, slots)]
    row_groups = sign_ref.shape[0]
    depth = row_groups * rows
    lane = lax.broadcasted_iota(jnp.int32, (rows, LANES), 1)
    row = lax.broadcasted_iota(jnp.int32, (rows, LANES), 0)
    flip = (
        lax.broadcasted_iota(jnp.int32, (LANES, LANES), 0)
        + lax.broadcasted_iota(jnp.int32, (LANES, LANES), 1)
        == LANES - 1
    ).astype(F32).astype(BF16)
    real_lane = lax.broadcasted_iota(jnp.int32, (LANES, LANES), 1) < LAGS

    def assemble(slot, part):
        loaded = [x_ref[d, part, slot].astype(F32) for d in range(sources)]
        raw = []
        for group in range(row_groups):
            blocks = []
            for block in range(BLOCKS):
                total = None
                for place in range(PER_ROW):
                    packet = group * PKTS + block * PER_ROW + place
                    shift = (place - packet // sources) * PKT % LANES
                    piece = loaded[packet % sources]
                    if shift:
                        piece = pltpu.roll(piece, shift, 1)
                    total = piece if total is None else jnp.where(lane >= place * PKT, piece, total)
                blocks.append(total)
            raw.append(blocks)
        raw.append([jnp.where(row == rows - 1, 0.0, pltpu.roll(raw[0][0], rows - 1, 0))])
        for group in range(row_groups):
            top = part * depth + group * rows
            for block in range(BLOCKS + 1):
                piece = raw[group][block] if block < BLOCKS else raw[group + 1][0]
                columns = slice(block * LANES, (block + 1) * LANES)
                both_ref[slot, top : top + rows, columns] = (piece * sign_ref[group]).astype(BF16)

    for slot in range(slots):
        assemble(slot, 0)
        assemble(slot, 1)
    for slot in range(slots):
        for block in range(BLOCKS + 1):
            columns = slice(block * LANES, (block + 1) * LANES)
            back = slice((BLOCKS - block) * LANES, (BLOCKS - block + 1) * LANES)
            turned = jnp.dot(both_ref[slot, :, columns], flip, preferred_element_type=F32)
            back_ref[slot, :, back] = turned.astype(BF16)
    for slot in range(slots):
        held = slice(slot * LANES, (slot + 1) * LANES)
        for block in range(BLOCKS):
            columns = slice(block * LANES, (block + 1) * LANES)
            base = both_ref[slot, :, columns]
            turned = jnp.concatenate([-base[depth:], base[:depth]], 0)
            first = (BLOCKS - 1 - block) * LANES
            gram = lax.dot_general(
                jnp.concatenate([base, turned], 1),
                back_ref[slot, :, first : first + 2 * LANES],
                (((0,), (0,)), ((), ())),
                preferred_element_type=F32,
            )
            real_lags = pltpu.roll(gram[:LANES], LANES + 1, 1, stride=1, stride_axis=0)
            imag_lags = pltpu.roll(gram[LANES:], LAGS + 1, 1, stride=1, stride_axis=0)
            lags = jnp.where(real_lane, imag_lags[:, :LANES], real_lags[:, :LANES])
            high = lags.astype(BF16)
            low = (lags - high.astype(F32)).astype(BF16)
            top = 2 * block * LANES
            lag_ref[top : top + LANES, held] = high
            lag_ref[top + LANES : top + 2 * LANES, held] = low
    gates = [gate_ref[:, b * LANES : (b + 1) * LANES] for b in range(BLOCKS)]
    gates = jnp.concatenate([gate for gate in gates for _ in range(2)], 1)
    sums = jnp.dot(gates, lag_ref[...], preferred_element_type=F32)
    for slot in range(slots):
        rows_of = (sums[:, slot * LANES : (slot + 1) * LANES] * scale).astype(BF16)
        sum_ref[slot] = jnp.dot(rows_of, flip, preferred_element_type=F32)
    for step, out_ref in enumerate(reversed(out_refs)):
        gates = out_ref.shape[1] * out_ref.shape[2]
        first = pl.multiple_of((chip ^ step) * gates, gates)
        out_ref[...] = sum_ref[:, pl.ds(first, gates), :].reshape(out_ref.shape).astype(BF16)


def lag_profiles(place, signs, gate_hot, pieces, sources, slots, scale):
    chips = sources // 2
    row_groups, rows, _ = signs.shape
    out = jax.ShapeDtypeStruct((slots, 2, GATES // sources, LANES), BF16)
    vmem = pl.BlockSpec(memory_space=pltpu.VMEM)
    return pl.pallas_call(
        functools.partial(lag_kernel, scale, len(pieces)),
        in_specs=[pl.BlockSpec(memory_space=pltpu.SMEM)] * 2 + [vmem] * (2 + len(pieces)),
        out_specs=[vmem] * chips,
        out_shape=[out] * chips,
        scratch_shapes=[
            pltpu.VMEM((sources, 2, slots, rows, LANES), BF16),
            pltpu.VMEM((slots, 2 * row_groups * rows, (BLOCKS + 1) * LANES), BF16),
            pltpu.VMEM((slots, 2 * row_groups * rows, (BLOCKS + 1) * LANES), BF16),
            pltpu.VMEM((2 * IPP_LEN, slots * LANES), BF16),
            pltpu.VMEM((slots, GATES, LANES), F32),
        ],
        compiler_params=pltpu.CompilerParams(vmem_limit_bytes=VMEM),
        name="lag_profiles",
    )(*place, signs, gate_hot, *pieces)


def gather_kernel(width, chip_ref, core_ref, *refs):
    pieces_in = refs[:-1]
    out_ref = refs[-1]
    chips = len(pieces_in) // 2
    beams = out_ref.shape[0]
    slots = pieces_in[0].shape[0]
    chip = chip_ref[0]
    core = core_ref[0]
    for index, ref in enumerate(reversed(pieces_in)):
        first = (chip ^ (index // 2)) * (beams - width) // (chips - 1)
        first += (core ^ (index % 2)) * (width - slots)
        out_ref[pl.ds(first, slots)] = ref[:, core].astype(F32)


def gather_beams(place, pieces, width, beams):
    gates = pieces[0].shape[2]
    vmem = pl.BlockSpec(memory_space=pltpu.VMEM)
    return pl.pallas_call(
        functools.partial(gather_kernel, width),
        in_specs=[pl.BlockSpec(memory_space=pltpu.SMEM)] * 2 + [vmem] * len(pieces),
        out_specs=vmem,
        out_shape=jax.ShapeDtypeStruct((beams, gates, LANES), F32),
        compiler_params=pltpu.CompilerParams(vmem_limit_bytes=VMEM),
        name="gather_beams",
    )(*place, *reversed(pieces))


def sign_rows(code_signs, periods, row_groups):
    signs = jnp.repeat((2 * code_signs - 1).astype(F32), BAUD_LEN, axis=1)
    signs = jnp.tile(signs, (periods // NCODES, 1))
    return signs.reshape(periods // row_groups, row_groups, LANES).transpose(1, 0, 2)


def gate_rows(gate_map):
    gates = jnp.repeat(gate_map, SEC_LEN)
    return (jnp.arange(GATES)[:, None] == gates[None, :]).astype(BF16)


def exchanged(block, axis, step):
    return lax.ppermute(block, axis, [(i, i ^ step) for i in range(lax.axis_size(axis))])


def spread(blocks):
    pieces = []
    for step, block in enumerate(blocks):
        block = exchanged(block, "tm", 2 * step) if step else block
        pieces += [block, exchanged(block, "tm", 1)]
    return pieces


def body(streams, beam_weights, code_signs, gate_map):
    groups = lax.axis_size("sub")
    sources = lax.axis_size("tm")
    chips = sources // 2
    beams = beam_weights.shape[1] // groups
    samples = streams.shape[2]
    width = -(-beams // chips)
    slots = -(-width // 2)
    periods = samples * sources // IPP_LEN
    scale = 1.0 / math.sqrt(periods * IPP_LEN / GATES)
    here = lax.axis_index("sub")
    chip = lax.axis_index("tm") // 2
    core = lax.axis_index("tm") % 2
    place = (chip.reshape(1), core.reshape(1))
    signs = sign_rows(code_signs, periods, sources // PER_ROW)
    gate_hot = gate_rows(gate_map)
    weights = pltpu.with_memory_space_constraint(beam_weights.transpose(1, 0, 2), pltpu.HBM)
    limit = 2 * streams.shape[1] * STREAM_MAX * WEIGHT_MAX
    gain = 2.0 ** math.floor(math.log2(60000.0 / limit))
    by_channel = streams.transpose(1, 0, 2)

    def first_of(owner):
        return owner * (beams - width) // (chips - 1)

    half = chips // 2
    count = max((half - 1) * (beams - width) // (chips - 1) + width, beams - first_of(half))
    low = chip < half
    pieces = [None] * sources
    for far in (True, False):
        start = jnp.where(low == far, beams - count, 0).astype(jnp.int32)
        partial = partial_beams(by_channel, weights, here, start, groups, count)
        total = partial[0]
        for step in range(groups - 1, 0, -1):
            came = exchanged((partial[step] * gain).astype(jnp.float16), "sub", step)
            total = total + came.astype(F32) * (1.0 / gain)
        total = total.astype(BF16)
        for step in range(half, chips) if far else range(half):
            place_of = first_of(chip ^ step) - start
            if far or not step:
                block = lax.dynamic_slice_in_dim(total, place_of, width, 1)
                block = exchanged(block, "tm", 2 * step) if step else block
                pieces[2 * step : 2 * step + 2] = [block, exchanged(block, "tm", 1)]
            else:
                for other in range(2):
                    first = place_of + (core ^ other) * (width - slots)
                    block = lax.dynamic_slice_in_dim(total, first, slots, 1)
                    pieces[2 * step + other] = exchanged(block, "tm", 2 * step + other)
    terms = lag_profiles(place, signs, gate_hot, pieces, sources, slots, scale)
    return gather_beams(place, spread(terms[::-1]), width, beams).transpose(1, 0, 2)


def solution(mesh):
    placed = (P(None, "sub", "tm"), P(None, None, "sub"), P(), P())
    return jax.shard_map(
        body, mesh=mesh, in_specs=placed, out_specs=P("tm", "sub", None), check_vma=False
    )
```

```python
import functools
import math

import jax
import jax.numpy as jnp
from jax import lax
from jax.experimental import pallas as pl
from jax.experimental.pallas import tpu as pltpu
from jax.sharding import PartitionSpec as P

PKT = 32
IPP_LEN = 512
LAGS = 64
NCODES = 32
BAUD_LEN = 8
SEC_LEN = 2
GATES = 128
LANES = 128
BLOCKS = IPP_LEN // LANES
PER_ROW = LANES // PKT
PKTS = IPP_LEN // PKT
STREAM_MAX = 6.0
WEIGHT_MAX = 0.09375
VMEM = 48 * 1024 * 1024
SLICE = 8
F32 = jnp.float32
BF16 = jnp.bfloat16


def beam_kernel(here_ref, start_ref, w_hbm, x_hbm, *refs):
    out_refs = refs[:-6]
    w_ref, x_ref, first_ref, second_ref, mixed_ref, sems = refs[-6:]
    groups = len(out_refs)
    depth = w_ref.shape[2]
    slices, _, _, width = x_ref.shape
    half = mixed_ref.shape[0] // 2
    count = out_refs[0].shape[1]
    w_copy = pltpu.make_async_copy(w_hbm, w_ref, sems.at[slices])
    w_copy.start()
    copies = []
    for index in range(slices):
        columns = pl.ds(index * width, width)
        copies.append(
            pltpu.make_async_copy(x_hbm.at[:, :, columns], x_ref.at[index], sems.at[index])
        )
        copies[-1].start()
    first_ref[...] = jnp.zeros_like(first_ref)
    second_ref[...] = jnp.zeros_like(second_ref)
    source = lax.broadcasted_iota(jnp.int32, (2 * LANES, 2 * LANES), 0)
    target = lax.broadcasted_iota(jnp.int32, (2 * LANES, 2 * LANES), 1)
    weave = source % LANES * 2 + source // LANES == target
    weave = weave.astype(F32).astype(BF16)
    w_copy.wait()
    for group in range(groups):
        owner = here_ref[0] ^ group
        chosen = pl.ds(owner * (w_ref.shape[0] // groups) + start_ref[0], count)
        weights = w_ref[chosen].astype(F32)
        real = weights[:, 0, :]
        imag = weights[:, 1, :]
        top = group * count
        first_ref[top : top + count, :depth] = real
        first_ref[half + top : half + top + count, :depth] = imag
        second_ref[top : top + count, :depth] = -imag
        second_ref[half + top : half + top + count, :depth] = real
    for block in range(first_ref.shape[1] // LANES):
        columns = slice(block * LANES, (block + 1) * LANES)
        pair = jnp.concatenate([first_ref[:, columns], second_ref[:, columns]], 1)
        woven = jnp.dot(pair.astype(BF16), weave, preferred_element_type=F32)
        mixed_ref[:, 2 * block * LANES : 2 * (block + 1) * LANES] = woven.astype(BF16)
    for index in range(slices):
        copies[index].wait()
        product = jnp.dot(
            mixed_ref[:, : 2 * depth],
            x_ref[index].reshape(2 * depth, width),
            preferred_element_type=F32,
        )
        rows = product.reshape(2 * half, width // LANES, LANES)
        place = slice(index * (width // LANES), (index + 1) * (width // LANES))
        for group, out_ref in enumerate(out_refs):
            top = group * count
            out_ref[0, :, place, :] = rows[top : top + count]
            out_ref[1, :, place, :] = rows[half + top : half + top + count]


def partial_beams(streams, weights, here, start, groups, count):
    depth, _, samples = streams.shape
    beams = groups * count
    width = SLICE * LANES
    rows = 2 * (-(-beams // 8) * 8)
    columns = -(-depth // LANES) * LANES
    return pl.pallas_call(
        beam_kernel,
        in_specs=[pl.BlockSpec(memory_space=pltpu.SMEM)] * 2
        + [pl.BlockSpec(memory_space=pltpu.HBM)] * 2,
        out_specs=[pl.BlockSpec(memory_space=pltpu.VMEM)] * groups,
        out_shape=[jax.ShapeDtypeStruct((2, count, samples // LANES, LANES), F32)] * groups,
        scratch_shapes=[
            pltpu.VMEM(weights.shape, BF16),
            pltpu.VMEM((samples // width, depth, 2, width), BF16),
            pltpu.VMEM((rows, columns), F32),
            pltpu.VMEM((rows, columns), F32),
            pltpu.VMEM((rows, 2 * columns), BF16),
            pltpu.SemaphoreType.DMA((samples // width + 1,)),
        ],
        compiler_params=pltpu.CompilerParams(vmem_limit_bytes=VMEM),
        cost_estimate=pl.CostEstimate(
            flops=8 * beams * depth * samples,
            bytes_accessed=4 * depth * samples + 8 * beams * samples,
            transcendentals=0,
        ),
        name="partial_beams",
    )(here.reshape(1), start.reshape(1), weights, streams)


def lag_kernel(scale, count, chip_ref, core_ref, sign_ref, gate_ref, *refs):
    pieces_in = refs[:count]
    out_refs = refs[count:-5]
    x_ref, both_ref, back_ref, lag_ref, sum_ref = refs[-5:]
    sources, _, slots, rows, _ = x_ref.shape
    chip = chip_ref[0]
    core = core_ref[0]
    taken = pieces_in[0].shape[1] - slots
    for index, ref in enumerate(pieces_in):
        source = 2 * (chip ^ (index // 2)) + (core ^ (index % 2))
        if ref.shape[1] == slots:
            x_ref[source] = ref[...]
        else:
            x_ref[source] = ref[:, pl.ds(core * taken, slots)]
    row_groups = sign_ref.shape[0]
    depth = row_groups * rows
    lane = lax.broadcasted_iota(jnp.int32, (rows, LANES), 1)
    row = lax.broadcasted_iota(jnp.int32, (rows, LANES), 0)
    flip = (
        lax.broadcasted_iota(jnp.int32, (LANES, LANES), 0)
        + lax.broadcasted_iota(jnp.int32, (LANES, LANES), 1)
        == LANES - 1
    ).astype(F32).astype(BF16)
    real_lane = lax.broadcasted_iota(jnp.int32, (LANES, LANES), 1) < LAGS

    def assemble(slot, part):
        loaded = [x_ref[d, part, slot].astype(F32) for d in range(sources)]
        raw = []
        for group in range(row_groups):
            blocks = []
            for block in range(BLOCKS):
                total = None
                for place in range(PER_ROW):
                    packet = group * PKTS + block * PER_ROW + place
                    shift = (place - packet // sources) * PKT % LANES
                    piece = loaded[packet % sources]
                    if shift:
                        piece = pltpu.roll(piece, shift, 1)
                    total = piece if total is None else jnp.where(lane >= place * PKT, piece, total)
                blocks.append(total)
            raw.append(blocks)
        raw.append([jnp.where(row == rows - 1, 0.0, pltpu.roll(raw[0][0], rows - 1, 0))])
        for group in range(row_groups):
            top = part * depth + group * rows
            for block in range(BLOCKS + 1):
                piece = raw[group][block] if block < BLOCKS else raw[group + 1][0]
                columns = slice(block * LANES, (block + 1) * LANES)
                both_ref[slot, top : top + rows, columns] = (piece * sign_ref[group]).astype(BF16)

    for slot in range(slots):
        assemble(slot, 0)
        assemble(slot, 1)
    for block in range(BLOCKS + 1):
        columns = slice(block * LANES, (block + 1) * LANES)
        back = slice((BLOCKS - block) * LANES, (BLOCKS - block + 1) * LANES)
        ahead = both_ref[:, :, columns].reshape(slots * 2 * depth, LANES)
        turned = jnp.dot(ahead, flip, preferred_element_type=F32).astype(BF16)
        back_ref[:, :, back] = turned.reshape(slots, 2 * depth, LANES)
    for slot in range(slots):
        held = slice(slot * LANES, (slot + 1) * LANES)
        for block in range(BLOCKS):
            columns = slice(block * LANES, (block + 1) * LANES)
            base = both_ref[slot, :, columns]
            turned = jnp.concatenate([-base[depth:], base[:depth]], 0)
            first = (BLOCKS - 1 - block) * LANES
            gram = lax.dot_general(
                jnp.concatenate([base, turned], 1),
                back_ref[slot, :, first : first + 2 * LANES],
                (((0,), (0,)), ((), ())),
                preferred_element_type=F32,
            )
            real_lags = pltpu.roll(gram[:LANES], LANES + 1, 1, stride=1, stride_axis=0)
            imag_lags = pltpu.roll(gram[LANES:], LAGS + 1, 1, stride=1, stride_axis=0)
            lags = jnp.where(real_lane, imag_lags[:, :LANES], real_lags[:, :LANES])
            high = lags.astype(BF16)
            low = (lags - high.astype(F32)).astype(BF16)
            top = 2 * block * LANES
            lag_ref[top : top + LANES, held] = high
            lag_ref[top + LANES : top + 2 * LANES, held] = low
    gates = [gate_ref[:, b * LANES : (b + 1) * LANES] for b in range(BLOCKS)]
    gates = jnp.concatenate([gate for gate in gates for _ in range(2)], 1)
    sums = jnp.dot(gates, lag_ref[...], preferred_element_type=F32)
    for slot in range(slots):
        rows_of = (sums[:, slot * LANES : (slot + 1) * LANES] * scale).astype(BF16)
        sum_ref[slot] = jnp.dot(rows_of, flip, preferred_element_type=F32)
    for step, out_ref in enumerate(reversed(out_refs)):
        gates = out_ref.shape[1] * out_ref.shape[2]
        first = pl.multiple_of((chip ^ step) * gates, gates)
        out_ref[...] = sum_ref[:, pl.ds(first, gates), :].reshape(out_ref.shape).astype(BF16)


def lag_profiles(place, signs, gate_hot, pieces, sources, slots, scale):
    chips = sources // 2
    row_groups, rows, _ = signs.shape
    out = jax.ShapeDtypeStruct((slots, 2, GATES // sources, LANES), BF16)
    vmem = pl.BlockSpec(memory_space=pltpu.VMEM)
    return pl.pallas_call(
        functools.partial(lag_kernel, scale, len(pieces)),
        in_specs=[pl.BlockSpec(memory_space=pltpu.SMEM)] * 2 + [vmem] * (2 + len(pieces)),
        out_specs=[vmem] * chips,
        out_shape=[out] * chips,
        scratch_shapes=[
            pltpu.VMEM((sources, 2, slots, rows, LANES), BF16),
            pltpu.VMEM((slots, 2 * row_groups * rows, (BLOCKS + 1) * LANES), BF16),
            pltpu.VMEM((slots, 2 * row_groups * rows, (BLOCKS + 1) * LANES), BF16),
            pltpu.VMEM((2 * IPP_LEN, slots * LANES), BF16),
            pltpu.VMEM((slots, GATES, LANES), F32),
        ],
        compiler_params=pltpu.CompilerParams(vmem_limit_bytes=VMEM),
        name="lag_profiles",
    )(*place, signs, gate_hot, *pieces)


def gather_kernel(width, chip_ref, core_ref, *refs):
    pieces_in = refs[:-1]
    out_ref = refs[-1]
    chips = len(pieces_in) // 2
    beams = out_ref.shape[0]
    slots = pieces_in[0].shape[0]
    chip = chip_ref[0]
    core = core_ref[0]
    for index, ref in enumerate(reversed(pieces_in)):
        first = (chip ^ (index // 2)) * (beams - width) // (chips - 1)
        first += (core ^ (index % 2)) * (width - slots)
        out_ref[pl.ds(first, slots)] = ref[:, core].astype(F32)


def gather_beams(place, pieces, width, beams):
    gates = pieces[0].shape[2]
    vmem = pl.BlockSpec(memory_space=pltpu.VMEM)
    return pl.pallas_call(
        functools.partial(gather_kernel, width),
        in_specs=[pl.BlockSpec(memory_space=pltpu.SMEM)] * 2 + [vmem] * len(pieces),
        out_specs=vmem,
        out_shape=jax.ShapeDtypeStruct((beams, gates, LANES), F32),
        compiler_params=pltpu.CompilerParams(vmem_limit_bytes=VMEM),
        name="gather_beams",
    )(*place, *reversed(pieces))


def sign_rows(code_signs, periods, row_groups):
    signs = jnp.repeat((2 * code_signs - 1).astype(F32), BAUD_LEN, axis=1)
    signs = jnp.tile(signs, (periods // NCODES, 1))
    return signs.reshape(periods // row_groups, row_groups, LANES).transpose(1, 0, 2)


def gate_rows(gate_map):
    gates = jnp.repeat(gate_map, SEC_LEN)
    return (jnp.arange(GATES)[:, None] == gates[None, :]).astype(BF16)


def exchanged(block, axis, step):
    return lax.ppermute(block, axis, [(i, i ^ step) for i in range(lax.axis_size(axis))])


def spread(blocks):
    pieces = []
    for step, block in enumerate(blocks):
        block = exchanged(block, "tm", 2 * step) if step else block
        pieces += [block, exchanged(block, "tm", 1)]
    return pieces


def body(streams, beam_weights, code_signs, gate_map):
    groups = lax.axis_size("sub")
    sources = lax.axis_size("tm")
    chips = sources // 2
    beams = beam_weights.shape[1] // groups
    samples = streams.shape[2]
    width = -(-beams // chips)
    slots = -(-width // 2)
    periods = samples * sources // IPP_LEN
    scale = 1.0 / math.sqrt(periods * IPP_LEN / GATES)
    here = lax.axis_index("sub")
    chip = lax.axis_index("tm") // 2
    core = lax.axis_index("tm") % 2
    place = (chip.reshape(1), core.reshape(1))
    signs = sign_rows(code_signs, periods, sources // PER_ROW)
    gate_hot = gate_rows(gate_map)
    weights = pltpu.with_memory_space_constraint(beam_weights.transpose(1, 0, 2), pltpu.HBM)
    limit = 2 * streams.shape[1] * STREAM_MAX * WEIGHT_MAX
    gain = 2.0 ** math.floor(math.log2(60000.0 / limit))
    by_channel = streams.transpose(1, 0, 2)

    def first_of(owner):
        return owner * (beams - width) // (chips - 1)

    half = chips // 2
    count = max((half - 1) * (beams - width) // (chips - 1) + width, beams - first_of(half))
    low = chip < half
    pieces = [None] * sources
    for far in (True, False):
        start = jnp.where(low == far, beams - count, 0).astype(jnp.int32)
        partial = partial_beams(by_channel, weights, here, start, groups, count)
        total = partial[0]
        for step in range(groups - 1, 0, -1):
            came = exchanged((partial[step] * gain).astype(jnp.float16), "sub", step)
            total = total + came.astype(F32) * (1.0 / gain)
        total = total.astype(BF16)
        for step in range(half, chips) if far else range(half):
            place_of = first_of(chip ^ step) - start
            if far or not step:
                block = lax.dynamic_slice_in_dim(total, place_of, width, 1)
                block = exchanged(block, "tm", 2 * step) if step else block
                pieces[2 * step : 2 * step + 2] = [block, exchanged(block, "tm", 1)]
            else:
                for other in range(2):
                    first = place_of + (core ^ other) * (width - slots)
                    block = lax.dynamic_slice_in_dim(total, first, slots, 1)
                    pieces[2 * step + other] = exchanged(block, "tm", 2 * step + other)
    terms = lag_profiles(place, signs, gate_hot, pieces, sources, slots, scale)
    return gather_beams(place, spread(terms[::-1]), width, beams).transpose(1, 0, 2)


def solution(mesh):
    placed = (P(None, "sub", "tm"), P(None, None, "sub"), P(), P())
    return jax.shard_map(
        body, mesh=mesh, in_specs=placed, out_specs=P("tm", "sub", None), check_vma=False
    )
```
